32 devices in a mesh: slab: 16 (over z, y, x), graph: 2 (over core).
Axes of the slice: x: 2, y: 2, z: 4, core: 2. Of those that a mesh axis runs over, the one named last changes fastest.
Arguments:
- nodes: bfloat16 [16384, 9, 128], P(('slab', 'graph')), may hold values from -6 to 6
- boundary: int32 [16, 2, 640], P('slab'), may hold values from 0 to 1023
- sources: int32 [81920], P(('slab', 'graph')), may hold values from 0 to 2303
- targets: int32 [81920], P(('slab', 'graph')), may hold values from 0 to 1023
- block_counts: int32 [16, 2], replicated, may hold values from 10 to 20, as said below
- wigner: float32 [35, 81920], P(None, ('slab', 'graph')), may hold values from -3 to 3
- radial: bfloat16 [81920, 128], P(('slab', 'graph')), may hold values from -6 to 6
- w_zero: bfloat16 [384, 384], replicated, may hold values from -0.3125 to 0.3125
- w_one: bfloat16 [2, 256, 256], replicated, may hold values from -0.25 to 0.25
- w_two: bfloat16 [2, 128, 128], replicated, may hold values from -0.375 to 0.375
Outputs:
- updated: bfloat16 [16384, 9, 128], P(('slab', 'graph'))
The draws below stay inside these ranges and needn't reach their ends.
Inputs may be any that keep to these rules, and one draw needn't show every extreme that they name: Slots of device (s, g) from block_counts[s, g] * 128 on are padding; every draw has some device with 20 live blocks.
All inputs are finite; a program needn't handle non-finite values.
Results may differ from the reference program's by a relative error of at most 0.0064.
Values may be sent and summed in bfloat16 or wider, within the bound.
No kernel may reach another device: no remote copies, remote signals or barrier semaphores. Data moves between devices by JAX's collectives and lax.ppermute only.
A program may use at most 64 MiB of HBM per device.

```python
import jax
import jax.numpy as jnp
from jax import lax

CHANNELS = 128
MAX_BLOCKS = 20
EDGE_BLOCK = 128
SLAB_ATOMS = 1024
FACE_ATOMS = 640
TABLE_ROWS = 2304
ATOMS = 16384
EDGES_DEV = 2560
EDGES = 81920
N_SLAB = 16
N_GRAPH = 2


def draw_block_counts(key, part):
    key_counts, key_busiest = jax.random.split(jax.random.fold_in(key, 11))
    least = max(1, MAX_BLOCKS // 2)
    total_devices = N_SLAB * N_GRAPH
    counts = jax.random.randint(key_counts, (total_devices,), least, MAX_BLOCKS + 1, dtype=jnp.int32)
    busiest = jax.random.randint(key_busiest, (), 0, total_devices, dtype=jnp.int32)
    counts = counts.at[busiest].set(MAX_BLOCKS)
    counts = counts.at[(busiest + 1) % total_devices].set(least)
    return counts.reshape(N_SLAB, N_GRAPH)


def with_ends(array, rng, low, high):
    longest = array.shape.index(max(array.shape))
    spots = []
    for shift in (0, 1):
        where = [jax.random.randint(jax.random.fold_in(rng, axis), (), 0, length) for axis, length in enumerate(array.shape)]
        where[longest] = (where[longest] + shift) % array.shape[longest]
        spots.append(tuple(where))
    return array.at[spots[0]].set(low).at[spots[1]].set(high)


def shard_levels(stream_key, dims, cuts, low, top_value):
    factor_of = 1.0
    for axis_at, parts in cuts:
        draws = jax.random.uniform(jax.random.fold_in(jax.random.fold_in(stream_key, 6), axis_at), (parts,), jnp.float32, low / len(cuts), top_value / len(cuts))
        factor_of = factor_of * jnp.repeat(jnp.exp(draws), dims[axis_at] // parts).reshape((-1,) + (1,) * (len(dims) - 1 - axis_at))
    return factor_of


def centred(key, shape, deviation, reach, shards=(), kind=jnp.bfloat16):
    loudness = shard_levels(key, shape, shards, -0.22, 0.18) if shards else 1.0
    entries = jax.random.normal(key, shape, jnp.float32) * deviation * loudness
    return jnp.minimum(jnp.maximum(entries, -reach), reach).astype(kind)


def setup_inputs(seed: int = 0) -> dict:
    key_of = jax.random.split(jax.random.key(seed), 11)
    return {
        "nodes": centred(key_of[0], (ATOMS, 9, CHANNELS), 1.0, 6.0, ((0, 32),)),
        "boundary": with_ends(jax.random.randint(key_of[1], (N_SLAB, 2, FACE_ATOMS), 0, SLAB_ATOMS), jax.random.fold_in(key_of[1], 1), 0, SLAB_ATOMS - 1).astype(jnp.int32),
        "sources": with_ends(jax.random.randint(key_of[2], (EDGES,), 0, TABLE_ROWS), jax.random.fold_in(key_of[2], 1), 0, TABLE_ROWS - 1).astype(jnp.int32),
        "targets": with_ends(jax.random.randint(key_of[3], (EDGES,), 0, SLAB_ATOMS), jax.random.fold_in(key_of[3], 1), 0, SLAB_ATOMS - 1).astype(jnp.int32),
        "block_counts": draw_block_counts(jax.random.fold_in(key_of[10], 71), 0),
        "wigner": centred(key_of[5], (35, EDGES), 0.5, 3.0, ((1, 32),), jnp.float32),
        "radial": centred(key_of[6], (EDGES, CHANNELS), 1.0, 6.0, ((0, 32),)),
        "w_zero": centred(key_of[7], (3 * CHANNELS, 3 * CHANNELS), (3 * CHANNELS) ** -0.5, 0.3125),
        "w_one": centred(key_of[8], (2, 2 * CHANNELS, 2 * CHANNELS), (4 * CHANNELS) ** -0.5, 0.25),
        "w_two": centred(key_of[9], (2, CHANNELS, CHANNELS), (2 * CHANNELS) ** -0.5, 0.375),
    }


message_scale = 0.2
wigner_blocks = ((0, 0, 1), (1, 1, 3), (10, 4, 5))


def rotate(coeffs, wig_rows, inverse):
    out_list = []
    for offset, first_coef, block_size in wigner_blocks:
        for row_index in range(block_size):
            summed = None
            for col_index in range(block_size):
                if inverse:
                    entry_index = offset + col_index * block_size + row_index
                else:
                    entry_index = offset + row_index * block_size + col_index
                product_term = wig_rows[entry_index][:, None] * coeffs[:, first_coef + col_index, :]
                summed = product_term if summed is None else summed + product_term
            out_list.append(summed)
    return jnp.stack(out_list, axis=1)


def build_pair(pair_weights):
    real_part = pair_weights[0]
    imag_part = pair_weights[1]
    top_half = jnp.concatenate([real_part, imag_part], axis=1)
    low_half = jnp.concatenate([-imag_part, real_part], axis=1)
    return jnp.concatenate([top_half, low_half], axis=0)


def mix_orders(rotated, w_zero, pair_one, pair_two):
    chan = rotated.shape[2]
    zero_in = jnp.concatenate([rotated[:, 0], rotated[:, 2], rotated[:, 6]], axis=1)
    zero_out = jnp.dot(zero_in, w_zero, preferred_element_type=jnp.float32)
    one_in = jnp.concatenate([rotated[:, 3], rotated[:, 7], rotated[:, 1], rotated[:, 5]], axis=1)
    one_out = jnp.dot(one_in, pair_one, preferred_element_type=jnp.float32)
    two_in = jnp.concatenate([rotated[:, 8], rotated[:, 4]], axis=1)
    two_out = jnp.dot(two_in, pair_two, preferred_element_type=jnp.float32)
    pieces = [zero_out[:, :chan], one_out[:, 2 * chan:3 * chan], zero_out[:, chan:2 * chan],
              one_out[:, :chan], two_out[:, chan:], one_out[:, 3 * chan:],
              zero_out[:, 2 * chan:], one_out[:, chan:2 * chan], two_out[:, :chan]]
    return jnp.stack(pieces, axis=1).astype(jnp.bfloat16)


def front(src_rows, wig_rows, rad_rows):
    turned = rotate(src_rows.astype(jnp.float32), wig_rows, False)
    return (turned * rad_rows.astype(jnp.float32)[:, None, :]).astype(jnp.bfloat16)


def finish(mixed, wig_rows, live_mask):
    turned = rotate(mixed.astype(jnp.float32), wig_rows, True)
    return (turned * live_mask[:, None, None]).astype(jnp.bfloat16)


def reference(nodes, boundary, sources, targets, block_counts, wigner, radial, w_zero, w_one, w_two):
    pair_one = build_pair(w_one)
    pair_two = build_pair(w_two)
    slabs = nodes.reshape(N_SLAB, SLAB_ATOMS, 9, CHANNELS)
    slots = jnp.arange(EDGES_DEV, dtype=jnp.int32)

    def one_device(totals, device):
        slab_index = device // N_GRAPH
        graph_index = device % N_GRAPH
        below_index = (slab_index + N_SLAB - 1) % N_SLAB
        above_index = (slab_index + 1) % N_SLAB
        lookup = jnp.concatenate([
            slabs[slab_index],
            jnp.take(slabs[below_index], boundary[below_index, 1], axis=0),
            jnp.take(slabs[above_index], boundary[above_index, 0], axis=0)], axis=0)
        begin = (device * EDGES_DEV).astype(jnp.int32)
        src_index = lax.dynamic_slice_in_dim(sources, begin, EDGES_DEV)
        tgt_index = lax.dynamic_slice_in_dim(targets, begin, EDGES_DEV)
        wig_rows = lax.dynamic_slice_in_dim(wigner, begin, EDGES_DEV, 1)
        rad_rows = lax.dynamic_slice_in_dim(radial, begin, EDGES_DEV, 0)
        live_mask = (slots < block_counts[slab_index, graph_index] * EDGE_BLOCK).astype(jnp.float32)
        mixed = mix_orders(front(jnp.take(lookup, src_index, axis=0), wig_rows, rad_rows), w_zero, pair_one, pair_two)
        messages = finish(mixed, wig_rows, live_mask)
        partial_value = jnp.zeros((SLAB_ATOMS, 9 * CHANNELS), jnp.float32).at[tgt_index].add(
            messages.reshape(EDGES_DEV, 9 * CHANNELS).astype(jnp.float32))
        row_start = (slab_index * SLAB_ATOMS).astype(jnp.int32)
        current = lax.dynamic_slice_in_dim(totals, row_start, SLAB_ATOMS, 0)
        return lax.dynamic_update_slice_in_dim(totals, current + partial_value, row_start, 0), None

    initial = jnp.zeros((ATOMS, 9 * CHANNELS), jnp.float32)
    totals, unused = lax.scan(one_device, initial, jnp.arange(N_SLAB * N_GRAPH, dtype=jnp.int32))
    return (totals * message_scale).astype(jnp.bfloat16).reshape(ATOMS, 9, CHANNELS)
```

```python
import functools

import jax
import jax.numpy as jnp
from jax import lax
from jax.experimental import pallas as pl
from jax.experimental.pallas import tpu as pltpu
from jax.sharding import PartitionSpec as P

EDGE_BLOCK = 128
BLK = 256
LANES = 128
LAST_CHUNK = 256
STRIDE = 1 << 16
MESSAGE_SCALE = 0.2
WIGNER_BLOCKS = ((0, 0, 1), (1, 1, 3), (10, 4, 5))
ORDER = (0, 2, 6, 3, 7, 1, 5, 8, 4)
AXES = ("slab", "graph")
WROWS = 48
HI, LO, IDX, FEATS = 128, 176, 224, 256
VMEM_LIMIT = 56 * 1024 * 1024

f32, bf16, i32 = jnp.float32, jnp.bfloat16, jnp.int32


def nn(a, b):
    return lax.dot_general(a, b, (((1,), (0,)), ((), ())), preferred_element_type=f32)


def nt(a, b):
    return lax.dot_general(a, b, (((1,), (1,)), ((), ())), preferred_element_type=f32)


def hot(index, rows):
    return jnp.where(
        lax.broadcasted_iota(i32, (rows, index.shape[1]), 0) == index, 1.0, 0.0
    ).astype(bf16)


def call(body, out_shape, *args, smem=(), smem_out=(), scratch=(), flops=0, aliases=None):
    outs = out_shape if isinstance(out_shape, (tuple, list)) else (out_shape,)
    spec = lambda on: pl.BlockSpec(memory_space=pltpu.SMEM if on else pltpu.VMEM)
    size = sum(a.size * a.dtype.itemsize for a in (*args, *outs))
    return pl.pallas_call(
        body,
        out_shape=out_shape,
        in_specs=[spec(i in smem) for i in range(len(args))],
        out_specs=[spec(i in smem_out) for i in range(len(outs))]
        if isinstance(out_shape, (tuple, list))
        else spec(0 in smem_out),
        scratch_shapes=list(scratch),
        input_output_aliases=aliases or {},
        compiler_params=pltpu.CompilerParams(vmem_limit_bytes=VMEM_LIMIT),
        cost_estimate=pl.CostEstimate(flops=flops, bytes_accessed=size, transcendentals=0),
    )(*args)


def pack_first(own, sib, index, table, face):
    half = own.shape[1]
    for c in range(own.shape[0]):
        rows = slice(c * LANES, (c + 1) * LANES)
        for i in range(0, half, LANES):
            table[rows, i : i + LANES] = own[c, i : i + LANES, :].T
            table[rows, half + i : half + i + LANES] = sib[c, i : i + LANES, :].T
    face[...] = nn(table[...], hot(index[...], 2 * half)).astype(bf16)


def pack_next(table, index, face):
    face[...] = nn(table[...], hot(index[...], table.shape[1])).astype(bf16)


def features(radial, wigner, sources, targets, w_zero, w_one, w_two, feats, wz, w1, w2, padded):
    edges = radial.shape[0]
    for i in range(0, edges, LANES):
        feats[0:LANES, i : i + LANES] = radial[i : i + LANES, :].T
    padded[...] = jnp.zeros(padded.shape, f32)
    padded[0 : wigner.shape[0], :] = wigner[...]
    value = padded[...]
    high = value.astype(bf16)
    feats[HI:LO, :] = high
    feats[LO:IDX, :] = (value - high.astype(f32)).astype(bf16)
    row = lax.broadcasted_iota(i32, (FEATS - IDX, edges), 0)
    src, tgt = sources[...], targets[...]
    digits = jnp.where(row == 0, src // 256, jnp.where(row == 1, src % 256, 0))
    digits = jnp.where(row == 2, tgt // 256, jnp.where(row == 3, tgt % 256, digits))
    feats[IDX:FEATS, :] = digits.astype(f32).astype(bf16)
    wz[...] = w_zero[...].T
    for weights, out in ((w_one, w1), (w_two, w2)):
        n = weights.shape[1]
        real, imag = weights[0].T, weights[1].T
        out[0:n, 0:n] = real
        out[0:n, n : 2 * n] = (-imag.astype(f32)).astype(bf16)
        out[n : 2 * n, 0:n] = imag
        out[n : 2 * n, n : 2 * n] = real


def places(slab, face, first, info, own, sib, pos_own, pos_sib, counts):
    g = info[0]
    rows = own.shape[0]
    at_zero = g == 0
    parts = []
    for which in range(2):
        src = jnp.where(at_zero == (which == 0), own[...], sib[...])
        edge = lax.broadcasted_iota(i32, (rows, LANES), 0) * LANES + lax.broadcasted_iota(
            i32, (rows, LANES), 1
        )
        parts.append(jnp.where(edge < info[1 + which] * EDGE_BLOCK, src, -1))
    src = jnp.concatenate(parts, axis=0)
    at = src - slab - face * g
    on_face = jnp.logical_and(src >= slab, jnp.logical_and(at >= 0, at < face))
    masks = (
        jnp.logical_and(src >= 0, src < slab),
        jnp.logical_and(on_face, at < first),
        jnp.logical_and(on_face, at >= first),
    )
    both = 2 * rows
    upper = (
        lax.broadcasted_iota(i32, (LANES, LANES), 0) < lax.broadcasted_iota(i32, (LANES, LANES), 1)
    ).astype(f32).astype(bf16)
    lower = (
        lax.broadcasted_iota(i32, (both, both), 1) < lax.broadcasted_iota(i32, (both, both), 0)
    ).astype(f32).astype(bf16)
    ones = jnp.ones((LANES, LANES), bf16)
    pos = jnp.full((both, LANES), -1, i32)
    for k, mask in enumerate(masks):
        member = mask.astype(f32)
        m16 = member.astype(bf16)
        before = nn(nn(lower, m16).astype(bf16), ones) + nn(m16, upper)
        pos = jnp.where(mask, before.astype(i32) + k * STRIDE, pos)
        counts[k] = jnp.sum(member).astype(i32)
    low, high = pos[0:rows], pos[rows:both]
    pos_own[...] = jnp.where(at_zero, low, high)
    pos_sib[...] = jnp.where(at_zero, high, low)


def blocks_of(info, counts):
    total = [(counts[k] + (BLK - 1)) // BLK for k in range(3)]
    mine = (total[0] + 1 - info[0]) // 2
    return mine, total[1], total[2]


def group(info, counts, feat_own, feat_sib, pos_own, pos_sib, out, hot_own, hot_sib):
    n0, n1, n2 = blocks_of(info, counts)
    g = info[0]

    def step(t, carry):
        base = jnp.where(
            t < n0,
            (2 * t + g) * BLK,
            jnp.where(t < n0 + n1, STRIDE + (t - n0) * BLK, 2 * STRIDE + (t - n0 - n1) * BLK),
        )
        want = lax.broadcasted_iota(i32, (BLK, LANES), 0) + base
        for pos, mask in ((pos_own, hot_own), (pos_sib, hot_sib)):
            for i in range(pos.shape[0]):
                mask[:, i * LANES : (i + 1) * LANES] = jnp.where(
                    pos[i : i + 1, :] == want, 1.0, 0.0
                ).astype(bf16)
        picked = nt(feat_own[...], hot_own[...]) + nt(feat_sib[...], hot_sib[...])
        out[t] = picked.astype(bf16)
        return carry

    lax.fori_loop(0, n0 + n1 + n2, step, 0)


def messages_of(kind, shift, info, counts, grouped, table, wz, w1, w2, acc, x, w, rot, mix, msg):
    n = blocks_of(info, counts)
    start = (0, n[0], n[0] + n[1])[kind]
    g = info[0]
    slab = acc.shape[0]
    half = slab // 2
    rows = table.shape[1]
    n_zero, n_one, n_two = wz.shape[0], w1.shape[0], w2.shape[0]
    slot = {c: i for i, c in enumerate(ORDER)}

    def one(b, carry):
        at = start + b
        w[...] = grouped[at, HI:LO, :].astype(f32) + grouped[at, LO:IDX, :].astype(f32)
        digits = grouped[at, IDX : IDX + 16, :].astype(f32)
        src = (digits[0:1] * 256.0 + digits[1:2]).astype(i32)
        tgt = (digits[2:3] * 256.0 + digits[3:4]).astype(i32)
        if kind == 0:
            src = src + half * g
            src = jnp.where(src >= slab, src - slab, src)
        else:
            src = src - shift(g)
        tgt = tgt + half * g
        tgt = jnp.where(tgt >= slab, tgt - slab, tgt)
        x[...] = nn(table[...], hot(src, rows))
        for q in range(0, LANES, 16):
            rad = grouped[at, q : q + 16, :].astype(f32)
            for offset, first, size in WIGNER_BLOCKS:
                for i in range(size):
                    total = None
                    for j in range(size):
                        k = offset + i * size + j
                        r = (first + j) * LANES + q
                        term = w[k : k + 1, :] * x[r : r + 16, :]
                        total = term if total is None else total + term
                    r = slot[first + i] * LANES + q
                    rot[r : r + 16, :] = (total * rad).astype(bf16)
        mix[0:n_zero, :] = nn(wz[...], rot[0:n_zero, :])
        mix[n_zero : n_zero + n_one, :] = nn(w1[...], rot[n_zero : n_zero + n_one, :])
        mix[n_zero + n_one :, :] = nn(w2[...], rot[n_zero + n_one :, :])
        for q in range(0, LANES, 16):
            for offset, first, size in WIGNER_BLOCKS:
                for i in range(size):
                    total = None
                    for j in range(size):
                        k = offset + j * size + i
                        r = slot[first + j] * LANES + q
                        term = w[k : k + 1, :] * mix[r : r + 16, :]
                        total = term if total is None else total + term
                    r = (first + i) * LANES + q
                    msg[r : r + 16, :] = total.astype(bf16)
        acc[...] += nt(hot(tgt, slab), msg[...])
        return carry

    lax.fori_loop(0, n[kind], one, 0)


def sum_slab(info, counts, grouped, table, wz, w1, w2, acc, *scratch):
    acc[...] = jnp.zeros(acc.shape, f32)
    messages_of(0, None, info, counts, grouped, table, wz, w1, w2, acc, *scratch)


def sum_face(shift, info, counts, grouped, table, wz, w1, w2, before, acc, *scratch):
    acc[...] = before[...]
    messages_of(1, shift, info, counts, grouped, table, wz, w1, w2, acc, *scratch)


def sum_last(shift, info, counts, grouped, table, wz, w1, w2, before, own, send, acc, *scratch):
    acc[...] = before[...]
    messages_of(2, shift, info, counts, grouped, table, wz, w1, w2, acc, *scratch)
    half = own.shape[1]
    for c in range(own.shape[0]):
        columns = slice(c * LANES, (c + 1) * LANES)
        own[c] = acc[0:half, columns]
        send[c] = acc[half : 2 * half, columns].astype(bf16)


def per_device(
    nodes, boundary, sources, targets, block_counts, wigner, radial, w_zero, w_one, w_two
):
    half, coefs, chan = nodes.shape
    slab, width = 2 * half, coefs * chan
    face = boundary.shape[2]
    last = min(LAST_CHUNK, face // 2)
    first = face - last
    edges = sources.shape[0]
    n_slab = lax.axis_size("slab")
    s, g = lax.axis_index("slab"), lax.axis_index("graph")
    sds = jax.ShapeDtypeStruct

    place = lambda i, j: (i % n_slab) * 2 + j
    swap = [(place(i, j), place(i, 1 - j)) for i in range(n_slab) for j in range(2)]
    ring = [(place(i, 0), place(i + 1, 0)) for i in range(n_slab)]
    ring += [(place(i, 1), place(i - 1, 1)) for i in range(n_slab)]
    send = lambda x, to: lax.ppermute(x, AXES, to)

    own = jnp.transpose(nodes, (1, 0, 2))
    sib = send(own, swap)
    sources_own = sources.reshape(-1, LANES)
    sources_sib = send(sources_own, swap)
    info = jnp.concatenate([jnp.stack([g.astype(i32)]), lax.dynamic_index_in_dim(block_counts, s, 0, False)])

    listed = lax.dynamic_index_in_dim(boundary[0], 1 - g, 0, True)
    listed = listed + half * g
    listed = jnp.where(listed >= slab, listed - slab, listed)

    feats, wz, w1, w2 = call(
        features,
        (
            sds((FEATS, edges), bf16),
            sds(w_zero.shape, bf16),
            sds((2 * w_one.shape[1],) * 2, bf16),
            sds((2 * w_two.shape[1],) * 2, bf16),
        ),
        radial, wigner, sources[None], targets[None], w_zero, w_one, w_two,
        scratch=[pltpu.VMEM((WROWS, edges), f32)],
    )
    feats_sib = send(feats, swap)

    table, face_first = call(
        pack_first,
        (sds((width, slab), bf16), sds((width, first), bf16)),
        own, sib, listed[:, :first],
        flops=2 * width * slab * first,
    )
    got_first = send(face_first, ring)
    face_last = call(
        pack_next, sds((width, last), bf16), table, listed[:, first:], flops=2 * width * slab * last
    )
    got_last = send(face_last, ring)

    pos_own, pos_sib, counts = call(
        functools.partial(places, slab, face, first),
        (sds(sources_own.shape, i32), sds(sources_own.shape, i32), sds((3,), i32)),
        info, sources_own, sources_sib,
        smem=(0,), smem_out=(2,),
    )
    n_blocks = (2 * edges + BLK - 1) // BLK + 3
    grouped = call(
        group,
        sds((n_blocks, FEATS, BLK), bf16),
        info, counts, feats, feats_sib, pos_own, pos_sib,
        smem=(0, 1),
        scratch=[pltpu.VMEM((BLK, edges), bf16)] * 2,
        flops=2 * FEATS * BLK * edges * n_blocks,
    )

    scratch = [
        pltpu.VMEM((width, BLK), f32),
        pltpu.VMEM((WROWS, BLK), f32),
        pltpu.VMEM((width, BLK), bf16),
        pltpu.VMEM((width, BLK), f32),
        pltpu.VMEM((width, BLK), bf16),
    ]
    acc = call(
        sum_slab,
        sds((slab, width), f32),
        info, counts, grouped, table, wz, w1, w2,
        smem=(0, 1), scratch=scratch, flops=10 * 2 * BLK * width * (2 * slab + 512),
    )
    acc = call(
        functools.partial(sum_face, lambda g: slab + face * g),
        sds((slab, width), f32),
        info, counts, grouped, got_first, wz, w1, w2, acc,
        smem=(0, 1), scratch=scratch, flops=6 * 2 * BLK * width * (slab + 1024), aliases={7: 0},
    )
    mine, theirs = call(
        functools.partial(sum_last, lambda g: slab + face * g + first),
        (sds((coefs, half, chan), f32), sds((coefs, half, chan), bf16)),
        info, counts, grouped, got_last, wz, w1, w2, acc,
        smem=(0, 1), scratch=[pltpu.VMEM((slab, width), f32)] + scratch,
        flops=4 * 2 * BLK * width * (slab + 1024),
    )
    total = mine + send(theirs, swap).astype(f32)
    return jnp.transpose((total * MESSAGE_SCALE).astype(bf16), (1, 0, 2))


def solution(mesh):
    both = P(AXES)
    return jax.shard_map(
        per_device,
        mesh=mesh,
        in_specs=(
            P(AXES, None, None),
            P("slab", None, None),
            both,
            both,
            P(),
            P(None, AXES),
            P(AXES, None),
            P(),
            P(),
            P(),
        ),
        out_specs=P(AXES, None, None),
        check_vma=False,
    )
```

```python
import functools

import jax
import jax.numpy as jnp
from jax import lax
from jax.experimental import pallas as pl
from jax.experimental.pallas import tpu as pltpu
from jax.sharding import PartitionSpec as P

EDGE_BLOCK = 128
BLK = 256
LANES = 128
LAST_CHUNK = 256
STRIDE = 1 << 16
MESSAGE_SCALE = 0.2
WIGNER_BLOCKS = ((0, 0, 1), (1, 1, 3), (10, 4, 5))
ORDER = (0, 2, 6, 3, 7, 1, 5, 8, 4)
AXES = ("slab", "graph")
WROWS = 48
HI, LO, IDX, FEATS = 128, 176, 224, 256
VMEM_LIMIT = 24 * 1024 * 1024

f32, bf16, i32 = jnp.float32, jnp.bfloat16, jnp.int32


def nn(a, b):
    return lax.dot_general(a, b, (((1,), (0,)), ((), ())), preferred_element_type=f32)


def nt(a, b):
    return lax.dot_general(a, b, (((1,), (1,)), ((), ())), preferred_element_type=f32)


def hot(index, rows):
    return jnp.where(
        lax.broadcasted_iota(i32, (rows, index.shape[1]), 0) == index, 1.0, 0.0
    ).astype(bf16)


def call(body, out_shape, *args, smem=(), smem_out=(), scratch=(), flops=0, aliases=None):
    outs = out_shape if isinstance(out_shape, (tuple, list)) else (out_shape,)
    spec = lambda on: pl.BlockSpec(memory_space=pltpu.SMEM if on else pltpu.VMEM)
    size = sum(a.size * a.dtype.itemsize for a in (*args, *outs)) if flops else 0
    return pl.pallas_call(
        body,
        out_shape=out_shape,
        in_specs=[spec(i in smem) for i in range(len(args))],
        out_specs=[spec(i in smem_out) for i in range(len(outs))]
        if isinstance(out_shape, (tuple, list))
        else spec(0 in smem_out),
        scratch_shapes=list(scratch),
        input_output_aliases=aliases or {},
        compiler_params=pltpu.CompilerParams(vmem_limit_bytes=VMEM_LIMIT),
        cost_estimate=pl.CostEstimate(flops=flops, bytes_accessed=size, transcendentals=0),
    )(*args)


def spot():
    return lax.axis_index("slab"), lax.axis_index("graph")


def listed(boundary, base):
    g = spot()[1]
    both = boundary[0]
    return jnp.where(g == 0, both[1:2], both[0:1]) - base


def transposed(rows, table):
    for c in range(rows.shape[0]):
        for i in range(0, rows.shape[1], LANES):
            table[c * LANES : (c + 1) * LANES, i : i + LANES] = rows[c, i : i + LANES, :].T


def pack_own(own, boundary, table, share):
    half = own.shape[1]
    transposed(own, table)
    share[...] = nn(table[...], hot(listed(boundary, half * spot()[1]), half)).astype(bf16)


def pack_first(sib, boundary, share, table, face):
    half, first = sib.shape[1], face.shape[1]
    transposed(sib, table)
    index = listed(boundary, half - half * spot()[1])[:, 0:first]
    face[...] = (nn(table[...], hot(index, half)) + share[:, 0:first].astype(f32)).astype(bf16)


def pack_last(table, boundary, share, face):
    half, first = table.shape[1], share.shape[1] - face.shape[1]
    index = listed(boundary, half - half * spot()[1])[:, first:]
    face[...] = (nn(table[...], hot(index, half)) + share[:, first:].astype(f32)).astype(bf16)


def features(radial, wigner, sources, targets, w_zero, w_one, w_two, feats, wz, w1, w2, padded):
    chunks, _, size = feats.shape
    padded[...] = jnp.zeros(padded.shape, f32)
    padded[0 : wigner.shape[0], :] = wigner[...]
    row = lax.broadcasted_iota(i32, (FEATS - IDX, LANES), 0)
    for j in range(chunks):
        value = padded[:, j * size : (j + 1) * size]
        high = value.astype(bf16)
        feats[j, HI:LO, :] = high
        feats[j, LO:IDX, :] = (value - high.astype(f32)).astype(bf16)
        for i in range(0, size, LANES):
            at = j * size + i
            feats[j, 0:LANES, i : i + LANES] = radial[at : at + LANES, :].T
            src = sources[at // LANES : at // LANES + 1, :]
            tgt = targets[at // LANES : at // LANES + 1, :]
            digits = jnp.where(row == 0, src // 256, jnp.where(row == 1, src % 256, 0))
            digits = jnp.where(row == 2, tgt // 256, jnp.where(row == 3, tgt % 256, digits))
            feats[j, IDX:FEATS, i : i + LANES] = digits.astype(f32).astype(bf16)
    wz[...] = w_zero[...].T
    for weights, out in ((w_one, w1), (w_two, w2)):
        n = weights.shape[1]
        real, imag = weights[0].T, weights[1].T
        out[0:n, 0:n] = real
        out[0:n, n : 2 * n] = (-imag.astype(f32)).astype(bf16)
        out[n : 2 * n, 0:n] = imag
        out[n : 2 * n, n : 2 * n] = real


def places(half, face, first, chunk, block_counts, own, sib, pos_own, pos_sib, ahead):
    s, g = spot()
    rows = own.shape[0]
    edge = lax.broadcasted_iota(i32, (rows, LANES), 0) * LANES + lax.broadcasted_iota(
        i32, (rows, LANES), 1
    )
    own_src = jnp.where(edge < block_counts[s, g] * EDGE_BLOCK, own[...], -1)
    sib_src = jnp.where(edge < block_counts[s, 1 - g] * EDGE_BLOCK, sib[...], -1)
    src = jnp.concatenate([own_src, sib_src], axis=0)
    near = src - half * g
    at = src - 2 * half - face * g
    on_face = jnp.logical_and(at >= 0, at < face)
    masks = (
        jnp.logical_and(src >= 0, jnp.logical_and(near >= 0, near < half)),
        jnp.logical_and(on_face, at < first),
        jnp.logical_and(on_face, at >= first),
    )
    both = 2 * rows
    upper = (
        lax.broadcasted_iota(i32, (LANES, LANES), 0) < lax.broadcasted_iota(i32, (LANES, LANES), 1)
    ).astype(f32).astype(bf16)
    lower = (
        lax.broadcasted_iota(i32, (both, both), 1) < lax.broadcasted_iota(i32, (both, both), 0)
    ).astype(f32).astype(bf16)
    ones = jnp.ones((LANES, LANES), bf16)
    pos = jnp.full((both, LANES), -1, i32)
    step = chunk // LANES
    for k, mask in enumerate(masks):
        member = mask.astype(f32)
        m16 = member.astype(bf16)
        before = nn(nn(lower, m16).astype(bf16), ones) + nn(m16, upper)
        pos = jnp.where(mask, before.astype(i32) + k * STRIDE, pos)
        total = 0
        for j in range(both // step):
            ahead[k, j] = total
            total = total + jnp.sum(member[j * step : (j + 1) * step]).astype(i32)
        ahead[k, both // step] = total
    pos_own[...] = pos[0:rows]
    pos_sib[...] = pos[rows:both]


def blocks_of(ahead):
    return [(ahead[k, ahead.shape[1] - 1] + (BLK - 1)) // BLK for k in range(3)]


def group(ahead, feat_own, feat_sib, pos_own, pos_sib, out):
    n = blocks_of(ahead)
    chunks, _, size = feat_own.shape
    for k in range(3):
        start = sum(n[:k]) if k else 0
        for part, (feat, pos) in enumerate(((feat_own, pos_own), (feat_sib, pos_sib))):

            def one_chunk(j, carry):
                low = ahead[k, part * chunks + j]
                high = ahead[k, part * chunks + j + 1]
                begin = low // BLK
                end = jnp.where(high > low, (high + BLK - 1) // BLK, begin)

                def one_block(b, carry):
                    want = lax.broadcasted_iota(i32, (BLK, LANES), 0) + (b * BLK + k * STRIDE)
                    per = size // LANES
                    mask = jnp.concatenate(
                        [
                            jnp.where(pos[pl.ds(j * per + i, 1), :] == want, 1.0, 0.0).astype(bf16)
                            for i in range(per)
                        ],
                        axis=1,
                    )
                    picked = nt(feat[j], mask)

                    @pl.when(low <= b * BLK)
                    def _():
                        out[start + b] = picked.astype(bf16)

                    @pl.when(low > b * BLK)
                    def _():
                        out[start + b] = (out[start + b].astype(f32) + picked).astype(bf16)

                    return carry

                return lax.fori_loop(begin, end, one_block, carry)

            lax.fori_loop(0, chunks, one_chunk, 0)


def messages_of(kind, shift, ahead, grouped, table, wz, w1, w2, acc, x, w, rot, mix, msg):
    n = blocks_of(ahead)
    start = (0, n[0], n[0] + n[1])[kind]
    g = spot()[1]
    slab = acc.shape[0]
    half = slab // 2
    rows = table.shape[1]
    n_zero, n_one, n_two = wz.shape[0], w1.shape[0], w2.shape[0]
    slot = {c: i for i, c in enumerate(ORDER)}

    def one(b, carry):
        at = start + b
        w[...] = grouped[at, HI:LO, :].astype(f32) + grouped[at, LO:IDX, :].astype(f32)
        digits = grouped[at, IDX : IDX + 16, :].astype(f32)
        src = (digits[0:1] * 256.0 + digits[1:2]).astype(i32)
        tgt = (digits[2:3] * 256.0 + digits[3:4]).astype(i32)
        src = src - shift(g)
        tgt = tgt + half * g
        tgt = jnp.where(tgt >= slab, tgt - slab, tgt)
        x[...] = nn(table[...], hot(src, rows))
        for q in range(0, LANES, 16):
            rad = grouped[at, q : q + 16, :].astype(f32)
            for offset, first, size in WIGNER_BLOCKS:
                for i in range(size):
                    total = None
                    for j in range(size):
                        k = offset + i * size + j
                        r = (first + j) * LANES + q
                        term = w[k : k + 1, :] * x[r : r + 16, :]
                        total = term if total is None else total + term
                    r = slot[first + i] * LANES + q
                    rot[r : r + 16, :] = (total * rad).astype(bf16)
        mix[0:n_zero, :] = nn(wz[...], rot[0:n_zero, :])
        mix[n_zero : n_zero + n_one, :] = nn(w1[...], rot[n_zero : n_zero + n_one, :])
        mix[n_zero + n_one :, :] = nn(w2[...], rot[n_zero + n_one :, :])
        for q in range(0, LANES, 16):
            for offset, first, size in WIGNER_BLOCKS:
                for i in range(size):
                    total = None
                    for j in range(size):
                        k = offset + j * size + i
                        r = slot[first + j] * LANES + q
                        term = w[k : k + 1, :] * mix[r : r + 16, :]
                        total = term if total is None else total + term
                    r = (first + i) * LANES + q
                    msg[r : r + 16, :] = total.astype(bf16)
        acc[...] += nt(hot(tgt, slab), msg[...])
        return carry

    lax.fori_loop(0, n[kind], one, 0)


def put_half(acc, base, part):
    half = part.shape[1]
    for c in range(part.shape[0]):
        part[c] = acc[base : base + half, c * LANES : (c + 1) * LANES].astype(part.dtype)


def sum_near(shift, ahead, grouped, table, wz, w1, w2, acc, *scratch):
    acc[...] = jnp.zeros(acc.shape, f32)
    messages_of(0, shift, ahead, grouped, table, wz, w1, w2, acc, *scratch)


def sum_first(shift, ahead, grouped, table, wz, w1, w2, before, mine, send, acc, *scratch):
    acc[...] = before[...]
    messages_of(1, shift, ahead, grouped, table, wz, w1, w2, acc, *scratch)
    put_half(acc, 0, mine)
    put_half(acc, mine.shape[1], send)


def sum_last(shift, ahead, grouped, table, wz, w1, w2, mine, send, acc, *scratch):
    acc[...] = jnp.zeros(acc.shape, f32)
    messages_of(2, shift, ahead, grouped, table, wz, w1, w2, acc, *scratch)
    put_half(acc, 0, mine)
    put_half(acc, mine.shape[1], send)


def per_device(
    nodes, boundary, sources, targets, block_counts, wigner, radial, w_zero, w_one, w_two
):
    half, coefs, chan = nodes.shape
    slab, width = 2 * half, coefs * chan
    face = boundary.shape[2]
    last = min(LAST_CHUNK, face // 2)
    first = face - last
    edges = sources.shape[0]
    chunk = next(c for c in (512, 256, LANES) if edges % c == 0)
    n_slab = lax.axis_size("slab")
    sds = jax.ShapeDtypeStruct

    place = lambda i, j: (i % n_slab) * 2 + j
    swap = [(place(i, j), place(i, 1 - j)) for i in range(n_slab) for j in range(2)]
    ring = [(place(i, 0), place(i + 1, 0)) for i in range(n_slab)]
    ring += [(place(i, 1), place(i - 1, 1)) for i in range(n_slab)]
    send = lambda x, to: lax.ppermute(x, AXES, to)

    own = jnp.transpose(nodes, (1, 0, 2))
    sib = send(own, swap)
    sources_own = sources.reshape(-1, LANES)
    sources_sib = send(sources_own, swap)

    table, share = call(
        pack_own,
        (sds((width, half), bf16), sds((width, face), bf16)),
        own, boundary,
        flops=2 * width * half * face,
    )
    table_sib, face_first = call(
        pack_first,
        (sds((width, half), bf16), sds((width, first), bf16)),
        sib, boundary, share,
        flops=2 * width * half * first,
    )
    got_first = send(face_first, ring)
    face_last = call(
        pack_last, sds((width, last), bf16), table_sib, boundary, share,
        flops=2 * width * half * last,
    )
    got_last = send(face_last, ring)

    radial, wigner, face_last = lax.optimization_barrier((radial, wigner, face_last))
    feats, wz, w1, w2 = call(
        features,
        (
            sds((edges // chunk, FEATS, chunk), bf16),
            sds(w_zero.shape, bf16),
            sds((2 * w_one.shape[1],) * 2, bf16),
            sds((2 * w_two.shape[1],) * 2, bf16),
        ),
        radial, wigner, sources_own, targets.reshape(-1, LANES), w_zero, w_one, w_two,
        scratch=[pltpu.VMEM((WROWS, edges), f32)],
    )
    feats_sib = send(feats, swap)
    pos_own, pos_sib, ahead = call(
        functools.partial(places, half, face, first, chunk),
        (
            sds(sources_own.shape, i32),
            sds(sources_own.shape, i32),
            sds((3, 2 * edges // chunk + 1), i32),
        ),
        block_counts, sources_own, sources_sib,
        smem=(0,), smem_out=(2,),
    )
    n_blocks = (2 * edges + BLK - 1) // BLK + 3
    grouped = call(
        group,
        sds((n_blocks, FEATS, BLK), bf16),
        ahead, feats, feats_sib, pos_own, pos_sib,
        smem=(0,),
    )

    scratch = [
        pltpu.VMEM((width, BLK), f32),
        pltpu.VMEM((WROWS, BLK), f32),
        pltpu.VMEM((width, BLK), bf16),
        pltpu.VMEM((width, BLK), f32),
        pltpu.VMEM((width, BLK), bf16),
    ]
    total = pltpu.VMEM((slab, width), f32)
    halves = (sds((coefs, half, chan), f32), sds((coefs, half, chan), bf16))
    near = call(
        functools.partial(sum_near, lambda g: half * g),
        sds((slab, width), f32),
        ahead, grouped, table, wz, w1, w2,
        smem=(0,), scratch=scratch,
    )
    mine, theirs = call(
        functools.partial(sum_first, lambda g: slab + face * g),
        halves,
        ahead, grouped, got_first, wz, w1, w2, near,
        smem=(0,), scratch=[total] + scratch,
    )
    mine_last, theirs_last = call(
        functools.partial(sum_last, lambda g: slab + face * g + first),
        halves,
        ahead, grouped, got_last, wz, w1, w2,
        smem=(0,), scratch=[total] + scratch,
    )
    early = mine + send(theirs, swap).astype(f32)
    full = early + mine_last + send(theirs_last, swap).astype(f32)
    return jnp.transpose((full * MESSAGE_SCALE).astype(bf16), (1, 0, 2))


def solution(mesh):
    both = P(AXES)
    return jax.shard_map(
        per_device,
        mesh=mesh,
        in_specs=(
            P(AXES, None, None),
            P("slab", None, None),
            both,
            both,
            P(),
            P(None, AXES),
            P(AXES, None),
            P(),
            P(),
            P(),
        ),
        out_specs=P(AXES, None, None),
        check_vma=False,
    )
```

```python
import functools

import jax
import jax.numpy as jnp
from jax import lax
from jax.experimental import pallas as pl
from jax.experimental.pallas import tpu as pltpu
from jax.sharding import PartitionSpec as P

EDGE_BLOCK = 128
BLK = 256
LANES = 128
LAST_CHUNK = 256
STRIDE = 1 << 16
MESSAGE_SCALE = 0.2
WIGNER_BLOCKS = ((0, 0, 1), (1, 1, 3), (10, 4, 5))
ORDER = (0, 2, 6, 3, 7, 1, 5, 8, 4)
AXES = ("slab", "graph")
WROWS = 48
HI, LO, IDX, FEATS = 128, 176, 224, 256
VMEM_LIMIT = 24 * 1024 * 1024

f32, bf16, i32 = jnp.float32, jnp.bfloat16, jnp.int32


def nn(a, b):
    return lax.dot_general(a, b, (((1,), (0,)), ((), ())), preferred_element_type=f32)


def nt(a, b):
    return lax.dot_general(a, b, (((1,), (1,)), ((), ())), preferred_element_type=f32)


def hot(index, rows):
    return jnp.where(
        lax.broadcasted_iota(i32, (rows, index.shape[1]), 0) == index, 1.0, 0.0
    ).astype(bf16)


def call(body, out_shape, *args, smem=(), hbm=(), smem_out=(), scratch=(), flops=0):
    outs = out_shape if isinstance(out_shape, (tuple, list)) else (out_shape,)
    args = [
        pltpu.with_memory_space_constraint(a, pltpu.HBM) if i in hbm else a
        for i, a in enumerate(args)
    ]
    spec = lambda on: pl.BlockSpec(memory_space=pltpu.SMEM if on else pltpu.VMEM)
    size = sum(a.size * a.dtype.itemsize for a in (*args, *outs)) if flops else 0
    return pl.pallas_call(
        body,
        out_shape=out_shape,
        in_specs=[
            pl.BlockSpec(memory_space=pltpu.HBM) if i in hbm else spec(i in smem)
            for i in range(len(args))
        ],
        out_specs=[spec(i in smem_out) for i in range(len(outs))]
        if isinstance(out_shape, (tuple, list))
        else spec(0 in smem_out),
        scratch_shapes=list(scratch),
        compiler_params=pltpu.CompilerParams(vmem_limit_bytes=VMEM_LIMIT),
        cost_estimate=pl.CostEstimate(flops=flops, bytes_accessed=size, transcendentals=0),
    )(*args)


def spot():
    return lax.axis_index("slab"), lax.axis_index("graph")


def listed(boundary, base):
    g = spot()[1]
    both = boundary[0]
    return jnp.where(g == 0, both[1:2], both[0:1]) - base


def transposed(rows, table):
    for c in range(rows.shape[0]):
        for i in range(0, rows.shape[1], LANES):
            table[c * LANES : (c + 1) * LANES, i : i + LANES] = rows[c, i : i + LANES, :].T


def pack_first(sib, rest, share, table, face):
    half, first = sib.shape[1], face.shape[1]
    transposed(sib, table)
    index = rest[:, 0:first]
    face[...] = (nn(table[...], hot(index, half)) + share[:, 0:first].astype(f32)).astype(bf16)


def pack_last(table, rest, share, face):
    half, first = table.shape[1], share.shape[1] - face.shape[1]
    index = rest[:, first:]
    face[...] = (nn(table[...], hot(index, half)) + share[:, first:].astype(f32)).astype(bf16)


def fetch(sources, targets, sems):
    copies = [
        pltpu.make_async_copy(src, dst, sems.at[i])
        for i, (src, dst) in enumerate(zip(sources, targets))
    ]
    for copy in copies:
        copy.start()
    return copies


def early(*refs):
    given, outs, held, (padded, sems) = refs[:6], refs[6:10], refs[10:16], refs[16:]
    table, share, rest, feats = outs
    copies = fetch(given, held, sems)
    own, boundary, radial, wigner, sources, targets = held
    half = own.shape[1]
    copies[0].wait()
    transposed(own, table)
    copies[1].wait()
    share[...] = nn(table[...], hot(listed(boundary, half * spot()[1]), half)).astype(bf16)
    rest[...] = listed(boundary, half - half * spot()[1])
    for copy in copies[2:]:
        copy.wait()
    chunks, _, size = feats.shape
    padded[...] = jnp.zeros(padded.shape, f32)
    padded[0 : wigner.shape[0], :] = wigner[...]
    row = lax.broadcasted_iota(i32, (FEATS - IDX, LANES), 0)
    for j in range(chunks):
        value = padded[:, j * size : (j + 1) * size]
        high = value.astype(bf16)
        feats[j, HI:LO, :] = high
        feats[j, LO:IDX, :] = (value - high.astype(f32)).astype(bf16)
        for i in range(0, size, LANES):
            at = j * size + i
            feats[j, 0:LANES, i : i + LANES] = radial[at : at + LANES, :].T
            src = sources[at // LANES : at // LANES + 1, :]
            tgt = targets[at // LANES : at // LANES + 1, :]
            digits = jnp.where(row == 0, src // 256, jnp.where(row == 1, src % 256, 0))
            digits = jnp.where(row == 2, tgt // 256, jnp.where(row == 3, tgt % 256, digits))
            feats[j, IDX:FEATS, i : i + LANES] = digits.astype(f32).astype(bf16)


def places(half, face, first, chunk, block_counts, own, sib, pos_own, pos_sib, ahead):
    s, g = spot()
    rows = own.shape[0]
    edge = lax.broadcasted_iota(i32, (rows, LANES), 0) * LANES + lax.broadcasted_iota(
        i32, (rows, LANES), 1
    )
    own_src = jnp.where(edge < block_counts[s, g] * EDGE_BLOCK, own[...], -1)
    sib_src = jnp.where(edge < block_counts[s, 1 - g] * EDGE_BLOCK, sib[...], -1)
    src = jnp.concatenate([own_src, sib_src], axis=0)
    near = src - half * g
    at = src - 2 * half - face * g
    on_face = jnp.logical_and(at >= 0, at < face)
    masks = (
        jnp.logical_and(src >= 0, jnp.logical_and(near >= 0, near < half)),
        jnp.logical_and(on_face, at < first),
        jnp.logical_and(on_face, at >= first),
    )
    both = 2 * rows
    upper = (
        lax.broadcasted_iota(i32, (LANES, LANES), 0) < lax.broadcasted_iota(i32, (LANES, LANES), 1)
    ).astype(f32).astype(bf16)
    lower = (
        lax.broadcasted_iota(i32, (both, both), 1) < lax.broadcasted_iota(i32, (both, both), 0)
    ).astype(f32).astype(bf16)
    ones = jnp.ones((LANES, LANES), bf16)
    pos = jnp.full((both, LANES), -1, i32)
    step = chunk // LANES
    for k, mask in enumerate(masks):
        member = mask.astype(f32)
        m16 = member.astype(bf16)
        before = nn(nn(lower, m16).astype(bf16), ones) + nn(m16, upper)
        pos = jnp.where(mask, before.astype(i32) + k * STRIDE, pos)
        total = 0
        for j in range(both // step):
            ahead[k, j] = total
            total = total + jnp.sum(member[j * step : (j + 1) * step]).astype(i32)
        ahead[k, both // step] = total
    pos_own[...] = pos[0:rows]
    pos_sib[...] = pos[rows:both]


def blocks_of(ahead):
    return [(ahead[k, ahead.shape[1] - 1] + (BLK - 1)) // BLK for k in range(3)]


def group(
    ahead, feat_own, feat_sib, pos_own, pos_sib, zero_given, one_given, two_given,
    out, wz, w1, w2,
    w_zero, w_one, w_two, sems,
):
    copies = fetch((zero_given, one_given, two_given), (w_zero, w_one, w_two), sems)
    n = blocks_of(ahead)
    chunks, _, size = feat_own.shape
    per = size // LANES
    first_tile = [0, 2 * n[0], 2 * (n[0] + n[1])]
    out[...] = jnp.zeros(out.shape, bf16)
    row = lax.broadcasted_iota(i32, (BLK, LANES), 0)

    for part, (feat, pos) in enumerate(((feat_own, pos_own), (feat_sib, pos_sib))):

        def add(j, k, low_tile, picked_rows):
            want = row + (low_tile * LANES + k * STRIDE)
            mask = jnp.concatenate(
                [jnp.where(r == want, 1.0, 0.0).astype(bf16) for r in picked_rows], axis=1
            )
            picked = nt(feat[j], mask).astype(bf16)
            for i in range(2):
                t = first_tile[k] + low_tile + i
                out[t] = out[t] + picked[:, i * LANES : (i + 1) * LANES]

        def one_chunk(j, carry):
            rows = [pos[pl.ds(j * per + i, 1), :] for i in range(per)]
            low = [ahead[k, part * chunks + j] // LANES for k in range(3)]
            for k in range(3):
                add(j, k, low[k], rows)
            for k in range(3):
                high = (ahead[k, part * chunks + j + 1] + (LANES - 1)) // LANES
                more = (high - low[k] + 1) // 2

                def again(i, carry):
                    add(j, k, low[k] + 2 * i, rows)
                    return carry

                lax.fori_loop(1, more, again, 0)
            return carry

        lax.fori_loop(0, chunks, one_chunk, 0)

    for copy in copies:
        copy.wait()
    wz[...] = w_zero[...].T
    for weights, out in ((w_one, w1), (w_two, w2)):
        n = weights.shape[1]
        real, imag = weights[0].T, weights[1].T
        out[0:n, 0:n] = real
        out[0:n, n : 2 * n] = (-imag.astype(f32)).astype(bf16)
        out[n : 2 * n, 0:n] = imag
        out[n : 2 * n, n : 2 * n] = real


def messages_of(
    kind, shift, ahead, grouped, table, wz, w1, w2, begin, end, acc, x, w, rot, mix, msg
):
    n = blocks_of(ahead)
    start = (0, n[0], n[0] + n[1])[kind]
    n = n[kind]
    g = spot()[1]
    slab, rows = acc.shape[0], table.shape[1]
    half = slab // 2
    n_zero, n_one = wz.shape[0], w1.shape[0]
    slot = {c: i for i, c in enumerate(ORDER)}

    def feature(b, low, high):
        return jnp.concatenate(
            [grouped[2 * (start + b) + i, low:high, :].astype(f32) for i in range(2)], axis=1
        )

    def number(b, row):
        digits = feature(b, IDX, IDX + 16)
        return (digits[row : row + 1] * 256.0 + digits[row + 1 : row + 2]).astype(i32)

    def gather(b):
        w[b % 2] = feature(b, HI, LO) + feature(b, LO, IDX)
        x[...] = nn(table[...], hot(number(b, 0) - shift(g), rows))

    def turn(b, source, at, inverse, q):
        for offset, first, size in WIGNER_BLOCKS:
            for i in range(size):
                total = None
                for j in range(size):
                    k = offset + (j * size + i if inverse else i * size + j)
                    r = at(first + j) * LANES + q
                    term = w[b % 2, k : k + 1, :] * source[r : r + 16, :]
                    total = term if total is None else total + term
                yield first + i, total

    def forth(b):
        for q in range(0, LANES, 16):
            rad = feature(b, q, q + 16)
            for c, total in turn(b, x, lambda c: c, False, q):
                r = slot[c] * LANES + q
                rot[r : r + 16, :] = (total * rad).astype(bf16)

    def blend():
        mix[0:n_zero, :] = nn(wz[...], rot[0:n_zero, :])
        mix[n_zero : n_zero + n_one, :] = nn(w1[...], rot[n_zero : n_zero + n_one, :])
        mix[n_zero + n_one :, :] = nn(w2[...], rot[n_zero + n_one :, :])

    def back(b):
        for q in range(0, LANES, 16):
            for c, total in turn(b, mix, lambda c: slot[c], True, q):
                msg[c * LANES + q : c * LANES + q + 16, :] = total.astype(bf16)

    def mask(b):
        tgt = number(b, 2) + half * g
        return hot(jnp.where(tgt >= slab, tgt - slab, tgt), slab)

    @pl.when(n > 0)
    def _():
        begin()
        gather(0)
        forth(0)
        blend()

        def one(b, carry):
            gather(b)
            back(b - 1)
            forth(b)
            acc[...] += nt(mask(b - 1), msg[...])
            blend()
            return carry

        lax.fori_loop(1, n, one, 0)
        back(n - 1)
        end(mask(n - 1), msg)

    @pl.when(n == 0)
    def _():
        begin()
        end(None, msg)


def add_to(acc):
    def end(mask, msg):
        if mask is not None:
            acc[...] += nt(mask, msg[...])

    return end


def finish(acc, mine, send, mask, msg):
    half, width = mine.shape[1], acc.shape[1]
    step = 3 * LANES
    for r in range(0, width, step):
        part = acc[:, r : r + step]
        if mask is not None:
            part = part + nt(mask, msg[r : r + step, :])
        for c in range(r // LANES, (r + step) // LANES):
            at = c * LANES - r
            send[c] = part[half:, at : at + LANES].astype(send.dtype)
            mine[c] = part[:half, at : at + LANES]


def sum_near(shift, ahead, grouped, table, wz, w1, w2, acc, *scratch):
    def begin():
        acc[...] = jnp.zeros(acc.shape, f32)

    messages_of(0, shift, ahead, grouped, table, wz, w1, w2, begin, add_to(acc), acc, *scratch)


def sum_first(shift, ahead, grouped, table, wz, w1, w2, before, acc, *scratch):
    def begin():
        acc[...] = before[...]

    messages_of(1, shift, ahead, grouped, table, wz, w1, w2, begin, add_to(acc), acc, *scratch)


def sum_last(shift, ahead, grouped, table, wz, w1, w2, before, mine, send, acc, *scratch):
    def begin():
        acc[...] = before[...]

    end = functools.partial(finish, acc, mine, send)
    messages_of(2, shift, ahead, grouped, table, wz, w1, w2, begin, end, acc, *scratch)


def per_device(
    nodes, boundary, sources, targets, block_counts, wigner, radial, w_zero, w_one, w_two
):
    half, coefs, chan = nodes.shape
    slab, width = 2 * half, coefs * chan
    face = boundary.shape[2]
    last = min(LAST_CHUNK, face // 2)
    first = face - last
    edges = sources.shape[0]
    chunk = next(c for c in (512, 256, LANES) if edges % c == 0)
    n_slab = lax.axis_size("slab")
    sds = jax.ShapeDtypeStruct

    place = lambda i, j: (i % n_slab) * 2 + j
    swap = [(place(i, j), place(i, 1 - j)) for i in range(n_slab) for j in range(2)]
    ring = [(place(i, 0), place(i + 1, 0)) for i in range(n_slab)]
    ring += [(place(i, 1), place(i - 1, 1)) for i in range(n_slab)]
    send = lambda x, to: lax.ppermute(x, AXES, to)

    own = jnp.transpose(nodes, (1, 0, 2))
    sib = send(own, swap)
    sources_own = sources.reshape(-1, LANES)
    sources_sib = send(sources_own, swap)

    given = (own, boundary, radial, wigner, sources_own, targets.reshape(-1, LANES))
    table, share, rest, feats = call(
        early,
        (
            sds((width, half), bf16),
            sds((width, face), bf16),
            sds((1, face), i32),
            sds((edges // chunk, FEATS, chunk), bf16),
        ),
        *given,
        hbm=range(6),
        scratch=[pltpu.VMEM(a.shape, a.dtype) for a in given]
        + [pltpu.VMEM((WROWS, edges), f32), pltpu.SemaphoreType.DMA((6,))],
    )
    sib, sources_sib, feats = lax.optimization_barrier((sib, sources_sib, feats))
    table_sib, face_first = call(
        pack_first,
        (sds((width, half), bf16), sds((width, first), bf16)),
        sib, rest, share,
        flops=2 * width * half * first,
    )
    got_first = send(face_first, ring)
    face_last = call(
        pack_last, sds((width, last), bf16), table_sib, rest, share,
        flops=2 * width * half * last,
    )
    got_last = send(face_last, ring)

    feats_sib = send(feats, swap)
    sources_sib, face_last = lax.optimization_barrier((sources_sib, face_last))
    pos_own, pos_sib, ahead = call(
        functools.partial(places, half, face, first, chunk),
        (
            sds(sources_own.shape, i32),
            sds(sources_own.shape, i32),
            sds((3, 2 * edges // chunk + 1), i32),
        ),
        block_counts, sources_own, sources_sib,
        smem=(0,), smem_out=(2,),
    )
    n_blocks = (2 * edges + BLK - 1) // BLK + 3
    grouped, wz, w1, w2 = call(
        group,
        (
            sds((2 * n_blocks + 2, FEATS, LANES), bf16),
            sds(w_zero.shape, bf16),
            sds((2 * w_one.shape[1],) * 2, bf16),
            sds((2 * w_two.shape[1],) * 2, bf16),
        ),
        ahead, feats, feats_sib, pos_own, pos_sib, w_zero, w_one, w_two,
        smem=(0,), hbm=(5, 6, 7),
        scratch=[pltpu.VMEM(a.shape, a.dtype) for a in (w_zero, w_one, w_two)]
        + [pltpu.SemaphoreType.DMA((3,))],
    )

    scratch = [
        pltpu.VMEM((width, BLK), f32),
        pltpu.VMEM((2, WROWS, BLK), f32),
        pltpu.VMEM((width, BLK), bf16),
        pltpu.VMEM((width, BLK), f32),
        pltpu.VMEM((width, BLK), bf16),
    ]
    total = pltpu.VMEM((slab, width), f32)
    halves = (sds((coefs, half, chan), f32), sds((coefs, half, chan), bf16))
    near = call(
        functools.partial(sum_near, lambda g: half * g),
        sds((slab, width), f32),
        ahead, grouped, table, wz, w1, w2,
        smem=(0,), scratch=scratch,
    )
    both = call(
        functools.partial(sum_first, lambda g: slab + face * g),
        sds((slab, width), f32),
        ahead, grouped, got_first, wz, w1, w2, near,
        smem=(0,), scratch=scratch,
    )
    mine, theirs = call(
        functools.partial(sum_last, lambda g: slab + face * g + first),
        halves,
        ahead, grouped, got_last, wz, w1, w2, both,
        smem=(0,), scratch=[total] + scratch, flops=4 * 2 * BLK * width * (slab + 1024),
    )
    full = mine + send(theirs, swap).astype(f32)
    return jnp.transpose((full * MESSAGE_SCALE).astype(bf16), (1, 0, 2))


def solution(mesh):
    both = P(AXES)
    return jax.shard_map(
        per_device,
        mesh=mesh,
        in_specs=(
            P(AXES, None, None),
            P("slab", None, None),
            both,
            both,
            P(),
            P(None, AXES),
            P(AXES, None),
            P(),
            P(),
            P(),
        ),
        out_specs=P(AXES, None, None),
        check_vma=False,
    )
```

```python
import functools

import jax
import jax.numpy as jnp
from jax import lax
from jax.experimental import pallas as pl
from jax.experimental.pallas import tpu as pltpu
from jax.sharding import PartitionSpec as P

EDGE_BLOCK = 128
BLK = 256
LANES = 128
LAST_CHUNK = 256
STRIDE = 1 << 16
ALL = 1 << 16
NEAR_BLOCKS = 3
MESSAGE_SCALE = 0.2
WIGNER_BLOCKS = ((0, 0, 1), (1, 1, 3), (10, 4, 5))
ORDER = (0, 2, 6, 3, 7, 1, 5, 8, 4)
AXES = ("slab", "graph")
WROWS = 48
HI, LO, IDX, FEATS = 128, 176, 224, 256

f32, bf16, i32 = jnp.float32, jnp.bfloat16, jnp.int32


def nn(a, b):
    return lax.dot_general(a, b, (((1,), (0,)), ((), ())), preferred_element_type=f32)


def nt(a, b):
    return lax.dot_general(a, b, (((1,), (1,)), ((), ())), preferred_element_type=f32)


def hot(index, rows):
    return jnp.where(
        lax.broadcasted_iota(i32, (rows, index.shape[1]), 0) == index, 1.0, 0.0
    ).astype(bf16)


def call(body, out_shape, *args, smem=(), hbm=(), smem_out=(), scratch=(), flops=0, vmem=8):
    outs = out_shape if isinstance(out_shape, (tuple, list)) else (out_shape,)
    args = [
        pltpu.with_memory_space_constraint(a, pltpu.HBM) if i in hbm else a
        for i, a in enumerate(args)
    ]
    spec = lambda on: pl.BlockSpec(memory_space=pltpu.SMEM if on else pltpu.VMEM)
    size = sum(a.size * a.dtype.itemsize for a in (*args, *outs)) if flops else 0
    return pl.pallas_call(
        body,
        out_shape=out_shape,
        in_specs=[
            pl.BlockSpec(memory_space=pltpu.HBM) if i in hbm else spec(i in smem)
            for i in range(len(args))
        ],
        out_specs=[spec(i in smem_out) for i in range(len(outs))]
        if isinstance(out_shape, (tuple, list))
        else spec(0 in smem_out),
        scratch_shapes=list(scratch),
        compiler_params=pltpu.CompilerParams(vmem_limit_bytes=vmem * 1024 * 1024),
        cost_estimate=pl.CostEstimate(flops=flops, bytes_accessed=size, transcendentals=0),
    )(*args)


def spot():
    return lax.axis_index("slab"), lax.axis_index("graph")


def listed(boundary, base):
    g = spot()[1]
    both = boundary[0]
    return jnp.where(g == 0, both[1:2], both[0:1]) - base


def transposed(rows, table):
    for c in range(rows.shape[0]):
        for i in range(0, rows.shape[1], LANES):
            table[c * LANES : (c + 1) * LANES, i : i + LANES] = rows[c, i : i + LANES, :].T


def pack_first(sib, rest, share, table, face):
    half, first = sib.shape[1], face.shape[1]
    transposed(sib, table)
    index = rest[:, 0:first]
    face[...] = (nn(table[...], hot(index, half)) + share[:, 0:first].astype(f32)).astype(bf16)


def pack_last(table, rest, share, face):
    half, first = table.shape[1], share.shape[1] - face.shape[1]
    index = rest[:, first:]
    face[...] = (nn(table[...], hot(index, half)) + share[:, first:].astype(f32)).astype(bf16)


def fetch(sources, targets, sems):
    copies = [
        pltpu.make_async_copy(src, dst, sems.at[i])
        for i, (src, dst) in enumerate(zip(sources, targets))
    ]
    for copy in copies:
        copy.start()
    return copies


def early(*refs):
    given, outs, held, (padded, sems) = refs[:6], refs[6:10], refs[10:16], refs[16:]
    table, share, rest, feats = outs
    copies = fetch(given, held, sems)
    own, boundary, radial, wigner, sources, targets = held
    half = own.shape[1]
    copies[0].wait()
    transposed(own, table)
    copies[1].wait()
    share[...] = nn(table[...], hot(listed(boundary, half * spot()[1]), half)).astype(bf16)
    rest[...] = listed(boundary, half - half * spot()[1])
    for copy in copies[2:]:
        copy.wait()
    chunks, _, size = feats.shape
    padded[...] = jnp.zeros(padded.shape, f32)
    padded[0 : wigner.shape[0], :] = wigner[...]
    row = lax.broadcasted_iota(i32, (FEATS - IDX, LANES), 0)
    for j in range(chunks):
        value = padded[:, j * size : (j + 1) * size]
        high = value.astype(bf16)
        feats[j, HI:LO, :] = high
        feats[j, LO:IDX, :] = (value - high.astype(f32)).astype(bf16)
        for i in range(0, size, LANES):
            at = j * size + i
            feats[j, 0:LANES, i : i + LANES] = radial[at : at + LANES, :].T
            src = sources[at // LANES : at // LANES + 1, :]
            tgt = targets[at // LANES : at // LANES + 1, :]
            digits = jnp.where(row == 0, src // 256, jnp.where(row == 1, src % 256, 0))
            digits = jnp.where(row == 2, tgt // 256, jnp.where(row == 3, tgt % 256, digits))
            feats[j, IDX:FEATS, i : i + LANES] = digits.astype(f32).astype(bf16)


def places(half, face, first, chunk, block_counts, own, sib, pos_own, pos_sib, ahead):
    s, g = spot()
    rows = own.shape[0]
    edge = lax.broadcasted_iota(i32, (rows, LANES), 0) * LANES + lax.broadcasted_iota(
        i32, (rows, LANES), 1
    )
    own_src = jnp.where(edge < block_counts[g, s] * EDGE_BLOCK, own[...], -1)
    sib_src = jnp.where(edge < block_counts[1 - g, s] * EDGE_BLOCK, sib[...], -1)
    src = jnp.concatenate([own_src, sib_src], axis=0)
    near = src - half * g
    at = src - 2 * half - face * g
    on_face = jnp.logical_and(at >= 0, at < face)
    masks = (
        jnp.logical_and(src >= 0, jnp.logical_and(near >= 0, near < half)),
        jnp.logical_and(on_face, at < first),
        jnp.logical_and(on_face, at >= first),
    )
    both = 2 * rows
    upper = (
        lax.broadcasted_iota(i32, (LANES, LANES), 0) < lax.broadcasted_iota(i32, (LANES, LANES), 1)
    ).astype(f32).astype(bf16)
    lower = (
        lax.broadcasted_iota(i32, (both, both), 1) < lax.broadcasted_iota(i32, (both, both), 0)
    ).astype(f32).astype(bf16)
    ones = jnp.ones((LANES, LANES), bf16)
    pos = jnp.full((both, LANES), -1, i32)
    step = chunk // LANES
    for k, mask in enumerate(masks):
        member = mask.astype(f32)
        m16 = member.astype(bf16)
        before = nn(nn(lower, m16).astype(bf16), ones) + nn(m16, upper)
        pos = jnp.where(mask, before.astype(i32) + k * STRIDE, pos)
        total = 0
        for j in range(both // step):
            ahead[k, j] = total
            total = total + jnp.sum(member[j * step : (j + 1) * step]).astype(i32)
        ahead[k, both // step] = total
    pos_own[...] = pos[0:rows]
    pos_sib[...] = pos[rows:both]


def blocks_of(ahead):
    return [(ahead[k, ahead.shape[1] - 1] + (BLK - 1)) // BLK for k in range(3)]


def group(
    ahead, feat_own, feat_sib, pos_own, pos_sib, zero_given, one_given, two_given,
    out, wz, w1, w2,
    w_zero, w_one, w_two, sems,
):
    copies = fetch((zero_given, one_given, two_given), (w_zero, w_one, w_two), sems)
    n = blocks_of(ahead)
    chunks, _, size = feat_own.shape
    per = size // LANES
    first_tile = [0, 2 * n[0], 2 * (n[0] + n[1])]
    out[...] = jnp.zeros(out.shape, bf16)
    row = lax.broadcasted_iota(i32, (BLK, LANES), 0)

    for part, (feat, pos) in enumerate(((feat_own, pos_own), (feat_sib, pos_sib))):

        def add(j, k, low_tile, picked_rows):
            want = row + (low_tile * LANES + k * STRIDE)
            mask = jnp.concatenate(
                [jnp.where(r == want, 1.0, 0.0).astype(bf16) for r in picked_rows], axis=1
            )
            picked = nt(feat[j], mask).astype(bf16)
            for i in range(2):
                t = first_tile[k] + low_tile + i
                out[t] = out[t] + picked[:, i * LANES : (i + 1) * LANES]

        def one_chunk(j, carry):
            rows = [pos[pl.ds(j * per + i, 1), :] for i in range(per)]
            low = [ahead[k, part * chunks + j] // LANES for k in range(3)]
            for k in range(3):
                add(j, k, low[k], rows)
            for k in range(3):
                high = (ahead[k, part * chunks + j + 1] + (LANES - 1)) // LANES
                more = (high - low[k] + 1) // 2

                def again(i, carry):
                    add(j, k, low[k] + 2 * i, rows)
                    return carry

                lax.fori_loop(1, more, again, 0)
            return carry

        lax.fori_loop(0, chunks, one_chunk, 0)

    for copy in copies:
        copy.wait()
    wz[...] = w_zero[...].T
    for weights, out in ((w_one, w1), (w_two, w2)):
        n = weights.shape[1]
        real, imag = weights[0].T, weights[1].T
        out[0:n, 0:n] = real
        out[0:n, n : 2 * n] = (-imag.astype(f32)).astype(bf16)
        out[n : 2 * n, 0:n] = imag
        out[n : 2 * n, n : 2 * n] = real


def messages_of(
    kind, part, shift, ahead, grouped, table, wz, w1, w2, begin, end, acc, x, w, rot, mix, msg
):
    n = blocks_of(ahead)
    start = (0, n[0], n[0] + n[1])[kind] + part[0]
    n = jnp.minimum(jnp.maximum(n[kind] - part[0], 0), part[1])
    g = spot()[1]
    slab, rows = acc.shape[0], table.shape[1]
    half = slab // 2
    n_zero, n_one = wz.shape[0], w1.shape[0]
    slot = {c: i for i, c in enumerate(ORDER)}

    def feature(b, low, high):
        return jnp.concatenate(
            [grouped[2 * (start + b) + i, low:high, :].astype(f32) for i in range(2)], axis=1
        )

    def number(b, row):
        digits = feature(b, IDX, IDX + 16)
        return (digits[row : row + 1] * 256.0 + digits[row + 1 : row + 2]).astype(i32)

    def gather(b):
        w[b % 2] = feature(b, HI, LO) + feature(b, LO, IDX)
        x[...] = nn(table[...], hot(number(b, 0) - shift(g), rows))

    def turn(b, source, at, inverse, q):
        for offset, first, size in WIGNER_BLOCKS:
            for i in range(size):
                total = None
                for j in range(size):
                    k = offset + (j * size + i if inverse else i * size + j)
                    r = at(first + j) * LANES + q
                    term = w[b % 2, k : k + 1, :] * source[r : r + 16, :]
                    total = term if total is None else total + term
                yield first + i, total

    def forth(b):
        for q in range(0, LANES, 16):
            rad = feature(b, q, q + 16)
            for c, total in turn(b, x, lambda c: c, False, q):
                r = slot[c] * LANES + q
                rot[r : r + 16, :] = (total * rad).astype(bf16)

    def blend():
        mix[0:n_zero, :] = nn(wz[...], rot[0:n_zero, :])
        mix[n_zero : n_zero + n_one, :] = nn(w1[...], rot[n_zero : n_zero + n_one, :])
        mix[n_zero + n_one :, :] = nn(w2[...], rot[n_zero + n_one :, :])

    def back(b):
        for q in range(0, LANES, 16):
            for c, total in turn(b, mix, lambda c: slot[c], True, q):
                msg[c * LANES + q : c * LANES + q + 16, :] = total.astype(bf16)

    def mask(b):
        tgt = number(b, 2) + half * g
        return hot(jnp.where(tgt >= slab, tgt - slab, tgt), slab)

    @pl.when(n > 0)
    def _():
        begin()
        gather(0)
        forth(0)
        blend()

        def one(b, carry):
            gather(b)
            back(b - 1)
            forth(b)
            acc[...] += nt(mask(b - 1), msg[...])
            blend()
            return carry

        lax.fori_loop(1, n, one, 0)
        back(n - 1)
        end(mask(n - 1), msg)

    @pl.when(n == 0)
    def _():
        begin()
        end(None, msg)


def add_to(acc):
    def end(mask, msg):
        if mask is not None:
            acc[...] += nt(mask, msg[...])

    return end


def finish(acc, mine, send, mask, msg):
    half, width = mine.shape[1], acc.shape[1]
    step = 3 * LANES
    for r in range(0, width, step):
        part = acc[:, r : r + step]
        if mask is not None:
            part = part + nt(mask, msg[r : r + step, :])
        for c in range(r // LANES, (r + step) // LANES):
            at = c * LANES - r
            send[c] = part[half:, at : at + LANES].astype(send.dtype)
            mine[c] = part[:half, at : at + LANES]


def sum_near(part, shift, ahead, grouped, table, wz, w1, w2, acc, *scratch):
    def begin():
        acc[...] = jnp.zeros(acc.shape, f32)

    messages_of(0, part, shift, ahead, grouped, table, wz, w1, w2, begin, add_to(acc), acc, *scratch)


def sum_more(kind, part, shift, ahead, grouped, table, wz, w1, w2, before, acc, *scratch):
    def begin():
        acc[...] = before[...]

    end = add_to(acc)
    messages_of(kind, part, shift, ahead, grouped, table, wz, w1, w2, begin, end, acc, *scratch)


def sum_last(shift, ahead, grouped, table, wz, w1, w2, before, mine, send, acc, *scratch):
    def begin():
        acc[...] = before[...]

    end = functools.partial(finish, acc, mine, send)
    messages_of(2, (0, ALL), shift, ahead, grouped, table, wz, w1, w2, begin, end, acc, *scratch)


def per_device(
    nodes, boundary, sources, targets, block_counts, wigner, radial, w_zero, w_one, w_two
):
    half, coefs, chan = nodes.shape
    slab, width = 2 * half, coefs * chan
    face = boundary.shape[2]
    last = min(LAST_CHUNK, face // 2)
    first = face - last
    edges = sources.shape[0]
    chunk = next(c for c in (512, 256, LANES) if edges % c == 0)
    n_slab = lax.axis_size("slab")
    sds = jax.ShapeDtypeStruct

    place = lambda i, j: (i % n_slab) * 2 + j
    swap = [(place(i, j), place(i, 1 - j)) for i in range(n_slab) for j in range(2)]
    ring = [(place(i, 0), place(i + 1, 0)) for i in range(n_slab)]
    ring += [(place(i, 1), place(i - 1, 1)) for i in range(n_slab)]
    send = lambda x, to: lax.ppermute(x, AXES, to)

    own = jnp.transpose(nodes, (1, 0, 2))
    sib = send(own, swap)
    sources_own = sources.reshape(-1, LANES)
    sources_sib = send(sources_own, swap)

    given = (own, boundary, radial, wigner, sources_own, targets.reshape(-1, LANES))
    table, share, rest, feats = call(
        early,
        (
            sds((width, half), bf16),
            sds((width, face), bf16),
            sds((1, face), i32),
            sds((edges // chunk, FEATS, chunk), bf16),
        ),
        *given,
        hbm=range(6), vmem=16,
        scratch=[pltpu.VMEM(a.shape, a.dtype) for a in given]
        + [pltpu.VMEM((WROWS, edges), f32), pltpu.SemaphoreType.DMA((6,))],
    )
    sib, sources_sib, feats = lax.optimization_barrier((sib, sources_sib, feats))
    table_sib, face_first = call(
        pack_first,
        (sds((width, half), bf16), sds((width, first), bf16)),
        sib, rest, share,
        flops=2 * width * half * first,
    )
    got_first = send(face_first, ring)
    feats_sib = send(feats, swap)
    face_last = call(
        pack_last, sds((width, last), bf16), table_sib, rest, share,
        flops=2 * width * half * last,
    )
    sources_sib, face_last = lax.optimization_barrier((sources_sib, face_last))
    pos_own, pos_sib, ahead = call(
        functools.partial(places, half, face, first, chunk),
        (
            sds(sources_own.shape, i32),
            sds(sources_own.shape, i32),
            sds((3, 2 * edges // chunk + 1), i32),
        ),
        block_counts.T, sources_own, sources_sib,
        smem=(0,), smem_out=(2,),
    )
    n_blocks = (2 * edges + BLK - 1) // BLK + 3
    grouped, wz, w1, w2 = call(
        group,
        (
            sds((2 * n_blocks + 2, FEATS, LANES), bf16),
            sds(w_zero.shape, bf16),
            sds((2 * w_one.shape[1],) * 2, bf16),
            sds((2 * w_two.shape[1],) * 2, bf16),
        ),
        ahead, feats, feats_sib, pos_own, pos_sib, w_zero, w_one, w_two,
        smem=(0,), hbm=(5, 6, 7), vmem=16,
        scratch=[pltpu.VMEM(a.shape, a.dtype) for a in (w_zero, w_one, w_two)]
        + [pltpu.SemaphoreType.DMA((3,))],
    )

    scratch = [
        pltpu.VMEM((width, BLK), f32),
        pltpu.VMEM((2, WROWS, BLK), f32),
        pltpu.VMEM((width, BLK), bf16),
        pltpu.VMEM((width, BLK), f32),
        pltpu.VMEM((width, BLK), bf16),
    ]
    total = pltpu.VMEM((slab, width), f32)
    halves = (sds((coefs, half, chan), f32), sds((coefs, half, chan), bf16))
    near = call(
        functools.partial(sum_near, (0, NEAR_BLOCKS), lambda g: half * g),
        sds((slab, width), f32),
        ahead, grouped, table, wz, w1, w2,
        smem=(0,), scratch=scratch, vmem=20,
    )
    near, face_last = lax.optimization_barrier((near, face_last))
    got_last = send(face_last, ring)
    near = call(
        functools.partial(sum_more, 0, (NEAR_BLOCKS, ALL), lambda g: half * g),
        sds((slab, width), f32),
        ahead, grouped, table, wz, w1, w2, near,
        smem=(0,), scratch=scratch, vmem=20,
    )
    both = call(
        functools.partial(sum_more, 1, (0, ALL), lambda g: slab + face * g),
        sds((slab, width), f32),
        ahead, grouped, got_first, wz, w1, w2, near,
        smem=(0,), scratch=scratch, vmem=20,
    )
    mine, theirs = call(
        functools.partial(sum_last, lambda g: slab + face * g + first),
        halves,
        ahead, grouped, got_last, wz, w1, w2, both,
        smem=(0,), scratch=[total] + scratch, vmem=20, flops=4 * 2 * BLK * width * (slab + 1024),
    )
    full = mine + send(theirs, swap).astype(f32)
    return jnp.transpose((full * MESSAGE_SCALE).astype(bf16), (1, 0, 2))


def solution(mesh):
    both = P(AXES)
    return jax.shard_map(
        per_device,
        mesh=mesh,
        in_specs=(
            P(AXES, None, None),
            P("slab", None, None),
            both,
            both,
            P(),
            P(None, AXES),
            P(AXES, None),
            P(),
            P(),
            P(),
        ),
        out_specs=P(AXES, None, None),
        check_vma=False,
    )
```

```python
import functools

import jax
import jax.numpy as jnp
from jax import lax
from jax.experimental import pallas as pl
from jax.experimental.pallas import tpu as pltpu
from jax.sharding import PartitionSpec as P

EDGE_BLOCK = 128
BLK = 256
LANES = 128
LAST_CHUNK = 256
STRIDE = 1 << 16
ALL = 1 << 16
NEAR_BLOCKS = 4
MESSAGE_SCALE = 0.2
WIGNER_BLOCKS = ((0, 0, 1), (1, 1, 3), (10, 4, 5))
ORDER = (0, 2, 6, 3, 7, 1, 5, 8, 4)
AXES = ("slab", "graph")
WROWS = 48
HI, LO, IDX, FEATS = 128, 176, 224, 256

f32, bf16, i32 = jnp.float32, jnp.bfloat16, jnp.int32


def nn(a, b):
    return lax.dot_general(a, b, (((1,), (0,)), ((), ())), preferred_element_type=f32)


def nt(a, b):
    return lax.dot_general(a, b, (((1,), (1,)), ((), ())), preferred_element_type=f32)


def hot(index, rows):
    return jnp.where(
        lax.broadcasted_iota(i32, (rows, index.shape[1]), 0) == index, 1.0, 0.0
    ).astype(bf16)


def call(body, out_shape, *args, smem=(), hbm=(), smem_out=(), hbm_out=False, scratch=(), flops=0, vmem=8):
    outs = out_shape if isinstance(out_shape, (tuple, list)) else (out_shape,)
    args = [
        pltpu.with_memory_space_constraint(a, pltpu.HBM) if i in hbm else a
        for i, a in enumerate(args)
    ]
    spec = lambda on: pl.BlockSpec(memory_space=pltpu.SMEM if on else pltpu.VMEM)
    size = sum(a.size * a.dtype.itemsize for a in (*args, *outs)) if flops else 0
    return pl.pallas_call(
        body,
        out_shape=out_shape,
        in_specs=[
            pl.BlockSpec(memory_space=pltpu.HBM) if i in hbm else spec(i in smem)
            for i in range(len(args))
        ],
        out_specs=[spec(i in smem_out) for i in range(len(outs))]
        if isinstance(out_shape, (tuple, list))
        else (pl.BlockSpec(memory_space=pltpu.HBM) if hbm_out else spec(0 in smem_out)),
        scratch_shapes=list(scratch),
        compiler_params=pltpu.CompilerParams(vmem_limit_bytes=vmem * 1024 * 1024),
        cost_estimate=pl.CostEstimate(flops=flops, bytes_accessed=size, transcendentals=0),
    )(*args)


def spot():
    return lax.axis_index("slab"), lax.axis_index("graph")


def listed(boundary, base):
    g = spot()[1]
    both = boundary[0]
    return jnp.where(g == 0, both[1:2], both[0:1]) - base


def transposed(rows, table):
    for c in range(rows.shape[0]):
        for i in range(0, rows.shape[1], LANES):
            table[c * LANES : (c + 1) * LANES, i : i + LANES] = rows[c, i : i + LANES, :].T


def pack_first(sib, rest, share, table, face):
    half, first = sib.shape[1], face.shape[1]
    transposed(sib, table)
    index = rest[:, 0:first]
    face[...] = (nn(table[...], hot(index, half)) + share[:, 0:first].astype(f32)).astype(bf16)


def pack_last(table, rest, share, face):
    half, first = table.shape[1], share.shape[1] - face.shape[1]
    index = rest[:, first:]
    face[...] = (nn(table[...], hot(index, half)) + share[:, first:].astype(f32)).astype(bf16)


def fetch(sources, targets, sems):
    copies = [
        pltpu.make_async_copy(src, dst, sems.at[i])
        for i, (src, dst) in enumerate(zip(sources, targets))
    ]
    for copy in copies:
        copy.start()
    return copies


def early(*refs):
    given, outs, held, (padded, sems) = refs[:6], refs[6:10], refs[10:16], refs[16:]
    table, share, rest, feats = outs
    copies = fetch(given, held, sems)
    own, boundary, radial, wigner, sources, targets = held
    half = own.shape[1]
    copies[0].wait()
    transposed(own, table)
    copies[1].wait()
    share[...] = nn(table[...], hot(listed(boundary, half * spot()[1]), half)).astype(bf16)
    rest[...] = listed(boundary, half - half * spot()[1])
    for copy in copies[2:]:
        copy.wait()
    chunks, _, size = feats.shape
    padded[...] = jnp.zeros(padded.shape, f32)
    padded[0 : wigner.shape[0], :] = wigner[...]
    row = lax.broadcasted_iota(i32, (FEATS - IDX, LANES), 0)
    for j in range(chunks):
        value = padded[:, j * size : (j + 1) * size]
        high = value.astype(bf16)
        feats[j, HI:LO, :] = high
        feats[j, LO:IDX, :] = (value - high.astype(f32)).astype(bf16)
        for i in range(0, size, LANES):
            at = j * size + i
            feats[j, 0:LANES, i : i + LANES] = radial[at : at + LANES, :].T
            src = sources[at // LANES : at // LANES + 1, :]
            tgt = targets[at // LANES : at // LANES + 1, :]
            digits = jnp.where(row == 0, src // 256, jnp.where(row == 1, src % 256, 0))
            digits = jnp.where(row == 2, tgt // 256, jnp.where(row == 3, tgt % 256, digits))
            feats[j, IDX:FEATS, i : i + LANES] = digits.astype(f32).astype(bf16)


def places(half, face, first, chunk, block_counts, own, sib, pos_own, pos_sib, ahead):
    s, g = spot()
    rows = own.shape[0]
    edge = lax.broadcasted_iota(i32, (rows, LANES), 0) * LANES + lax.broadcasted_iota(
        i32, (rows, LANES), 1
    )
    own_src = jnp.where(edge < block_counts[g, s] * EDGE_BLOCK, own[...], -1)
    sib_src = jnp.where(edge < block_counts[1 - g, s] * EDGE_BLOCK, sib[...], -1)
    src = jnp.concatenate([own_src, sib_src], axis=0)
    near = src - half * g
    at = src - 2 * half - face * g
    on_face = jnp.logical_and(at >= 0, at < face)
    masks = (
        jnp.logical_and(src >= 0, jnp.logical_and(near >= 0, near < half)),
        jnp.logical_and(on_face, at < first),
        jnp.logical_and(on_face, at >= first),
    )
    both = 2 * rows
    upper = (
        lax.broadcasted_iota(i32, (LANES, LANES), 0) < lax.broadcasted_iota(i32, (LANES, LANES), 1)
    ).astype(f32).astype(bf16)
    lower = (
        lax.broadcasted_iota(i32, (both, both), 1) < lax.broadcasted_iota(i32, (both, both), 0)
    ).astype(f32).astype(bf16)
    ones = jnp.ones((LANES, LANES), bf16)
    pos = jnp.full((both, LANES), -1, i32)
    step = chunk // LANES
    for k, mask in enumerate(masks):
        member = mask.astype(f32)
        m16 = member.astype(bf16)
        before = nn(nn(lower, m16).astype(bf16), ones) + nn(m16, upper)
        pos = jnp.where(mask, before.astype(i32) + k * STRIDE, pos)
        total = 0
        for j in range(both // step):
            ahead[k, j] = total
            total = total + jnp.sum(member[j * step : (j + 1) * step]).astype(i32)
        ahead[k, both // step] = total
    pos_own[...] = pos[0:rows]
    pos_sib[...] = pos[rows:both]


def blocks_of(ahead):
    return [(ahead[k, ahead.shape[1] - 1] + (BLK - 1)) // BLK for k in range(3)]


def group(
    ahead, feat_own, feat_sib, pos_own, pos_sib, zero_given, one_given, two_given,
    out, wz, w1, w2,
    w_zero, w_one, w_two, sems,
):
    copies = fetch((zero_given, one_given, two_given), (w_zero, w_one, w_two), sems)
    n = blocks_of(ahead)
    chunks, _, size = feat_own.shape
    per = size // LANES
    first_tile = [0, 2 * n[0], 2 * (n[0] + n[1])]
    out[...] = jnp.zeros(out.shape, bf16)
    row = lax.broadcasted_iota(i32, (BLK, LANES), 0)

    for part, (feat, pos) in enumerate(((feat_own, pos_own), (feat_sib, pos_sib))):

        def add(j, k, low_tile, picked_rows):
            want = row + (low_tile * LANES + k * STRIDE)
            mask = jnp.concatenate(
                [jnp.where(r == want, 1.0, 0.0).astype(bf16) for r in picked_rows], axis=1
            )
            picked = nt(feat[j], mask).astype(bf16)
            for i in range(2):
                t = first_tile[k] + low_tile + i
                out[t] = out[t] + picked[:, i * LANES : (i + 1) * LANES]

        def one_chunk(j, carry):
            rows = [pos[pl.ds(j * per + i, 1), :] for i in range(per)]
            low = [ahead[k, part * chunks + j] // LANES for k in range(3)]
            for k in range(3):
                add(j, k, low[k], rows)
            for k in range(3):
                high = (ahead[k, part * chunks + j + 1] + (LANES - 1)) // LANES
                more = (high - low[k] + 1) // 2

                def again(i, carry):
                    add(j, k, low[k] + 2 * i, rows)
                    return carry

                lax.fori_loop(1, more, again, 0)
            return carry

        lax.fori_loop(0, chunks, one_chunk, 0)

    for copy in copies:
        copy.wait()
    wz[...] = w_zero[...].T
    for weights, out in ((w_one, w1), (w_two, w2)):
        n = weights.shape[1]
        real, imag = weights[0].T, weights[1].T
        out[0:n, 0:n] = real
        out[0:n, n : 2 * n] = (-imag.astype(f32)).astype(bf16)
        out[n : 2 * n, 0:n] = imag
        out[n : 2 * n, n : 2 * n] = real


def features_of(grouped, block, low, high):
    tiles = [grouped[2 * block + i, low:high, :].astype(f32) for i in range(2)]
    return jnp.concatenate(tiles, axis=1)


def number(grouped, block, row):
    digits = features_of(grouped, block, IDX, IDX + 16)
    return (digits[row : row + 1] * 256.0 + digits[row + 1 : row + 2]).astype(i32)


def mask_of(grouped, block, half, base, rows):
    tgt = number(grouped, block, 2) + half * spot()[1]
    return hot(jnp.where(tgt >= 2 * half, tgt - 2 * half, tgt) - base, rows)


def messages_of(
    kind, part, shift, ahead, grouped, table, wz, w1, w2, begin, spread, end, msgs, x, w, rot, mix
):
    n = blocks_of(ahead)
    start = (0, n[0], n[0] + n[1])[kind] + part[0]
    n = jnp.minimum(jnp.maximum(n[kind] - part[0], 0), part[1])
    g = spot()[1]
    rows = table.shape[1]
    n_zero, n_one = wz.shape[0], w1.shape[0]
    slot = {c: i for i, c in enumerate(ORDER)}

    feature = lambda b, low, high: features_of(grouped, start + b, low, high)
    slot_of = lambda b: b if msgs.shape[0] > 1 else 0

    def gather(b):
        w[b % 2] = feature(b, HI, LO) + feature(b, LO, IDX)
        x[...] = nn(table[...], hot(number(grouped, start + b, 0) - shift(g), rows))

    def turn(b, source, at, inverse, q):
        for offset, first, size in WIGNER_BLOCKS:
            for i in range(size):
                total = None
                for j in range(size):
                    k = offset + (j * size + i if inverse else i * size + j)
                    r = at(first + j) * LANES + q
                    term = w[b % 2, k : k + 1, :] * source[r : r + 16, :]
                    total = term if total is None else total + term
                yield first + i, total

    def forth(b):
        for q in range(0, LANES, 16):
            rad = feature(b, q, q + 16)
            for c, total in turn(b, x, lambda c: c, False, q):
                r = slot[c] * LANES + q
                rot[r : r + 16, :] = (total * rad).astype(bf16)

    def blend():
        mix[0:n_zero, :] = nn(wz[...], rot[0:n_zero, :])
        mix[n_zero : n_zero + n_one, :] = nn(w1[...], rot[n_zero : n_zero + n_one, :])
        mix[n_zero + n_one :, :] = nn(w2[...], rot[n_zero + n_one :, :])

    def back(b):
        for q in range(0, LANES, 16):
            for c, total in turn(b, mix, lambda c: slot[c], True, q):
                r = c * LANES + q
                msgs[slot_of(b), r : r + 16, :] = total.astype(bf16)

    @pl.when(n > 0)
    def _():
        begin()
        gather(0)
        forth(0)
        blend()

        def one(b, carry):
            gather(b)
            back(b - 1)
            forth(b)
            spread(start + b - 1, slot_of(b - 1))
            blend()
            return carry

        lax.fori_loop(1, n, one, 0)
        back(n - 1)
        end(start + n - 1, slot_of(n - 1))

    @pl.when(n == 0)
    def _():
        begin()
        end(None, 0)


def add_to(acc, grouped, msgs, base=0):
    half = acc.shape[0] if base else acc.shape[0] // 2

    def spread(block, at):
        acc[...] += nt(mask_of(grouped, block, half, base, acc.shape[0]), msgs[at])

    def end(block, at):
        if block is not None:
            spread(block, at)

    return spread, end


def sum_near(part, shift, ahead, grouped, table, wz, w1, w2, acc, msgs, *scratch):
    def begin():
        acc[...] = jnp.zeros(acc.shape, f32)

    spread, end = add_to(acc, grouped, msgs)
    messages_of(
        0, part, shift, ahead, grouped, table, wz, w1, w2, begin, spread, end, msgs, *scratch
    )


def sum_more(kind, part, shift, ahead, grouped, table, wz, w1, w2, before, acc, msgs, *scratch):
    def begin():
        acc[...] = before[...]

    spread, end = add_to(acc, grouped, msgs)
    messages_of(
        kind, part, shift, ahead, grouped, table, wz, w1, w2, begin, spread, end, msgs, *scratch
    )


def sum_theirs(shift, ahead, grouped, table, wz, w1, w2, before, theirs, msgs, acc, *scratch):
    half, width = acc.shape

    def begin():
        acc[...] = before[half:, :]

    spread = add_to(acc, grouped, msgs, half)[0]

    def end(block, at):
        step = 3 * LANES
        for r in range(0, width, step):
            part = acc[:, r : r + step]
            if block is not None:
                mask = mask_of(grouped, block, half, half, half)
                part = part + nt(mask, msgs[at, r : r + step, :])
            for c in range(step // LANES):
                theirs[r // LANES + c] = part[:, c * LANES : (c + 1) * LANES].astype(bf16)

    messages_of(
        2, (0, ALL), shift, ahead, grouped, table, wz, w1, w2, begin, spread, end, msgs, *scratch
    )


def sum_mine(ahead, grouped, msgs, before, mine, acc):
    half = acc.shape[0]
    n = blocks_of(ahead)
    acc[...] = before[0:half, :]

    def one(b, carry):
        acc[...] += nt(mask_of(grouped, n[0] + n[1] + b, half, 0, half), msgs[b])
        return carry

    lax.fori_loop(0, n[2], one, 0)
    for c in range(mine.shape[0]):
        mine[c] = acc[:, c * LANES : (c + 1) * LANES]


def total_of(mine, theirs, out, held, sems):
    copies = []
    for c in range(mine.shape[0]):
        value = (mine[c] + theirs[c].astype(f32)) * MESSAGE_SCALE
        held[c] = value.astype(bf16)
        copies.append(pltpu.make_async_copy(held.at[c], out.at[c], sems.at[c]))
        copies[-1].start()
    for copy in copies:
        copy.wait()


def per_device(
    nodes, boundary, sources, targets, block_counts, wigner, radial, w_zero, w_one, w_two
):
    half, coefs, chan = nodes.shape
    slab, width = 2 * half, coefs * chan
    face = boundary.shape[2]
    last = min(LAST_CHUNK, face // 2)
    first = face - last
    edges = sources.shape[0]
    chunk = next(c for c in (512, 256, LANES) if edges % c == 0)
    n_slab = lax.axis_size("slab")
    sds = jax.ShapeDtypeStruct

    place = lambda i, j: (i % n_slab) * 2 + j
    swap = [(place(i, j), place(i, 1 - j)) for i in range(n_slab) for j in range(2)]
    ring = [(place(i, 0), place(i + 1, 0)) for i in range(n_slab)]
    ring += [(place(i, 1), place(i - 1, 1)) for i in range(n_slab)]
    send = lambda x, to: lax.ppermute(x, AXES, to)

    own = jnp.transpose(nodes, (1, 0, 2))
    sib = send(own, swap)
    sources_own = sources.reshape(-1, LANES)
    sources_sib = send(sources_own, swap)

    given = (own, boundary, radial, wigner, sources_own, targets.reshape(-1, LANES))
    table, share, rest, feats = call(
        early,
        (
            sds((width, half), bf16),
            sds((width, face), bf16),
            sds((1, face), i32),
            sds((edges // chunk, FEATS, chunk), bf16),
        ),
        *given,
        hbm=range(6), vmem=16,
        scratch=[pltpu.VMEM(a.shape, a.dtype) for a in given]
        + [pltpu.VMEM((WROWS, edges), f32), pltpu.SemaphoreType.DMA((6,))],
    )
    sib, sources_sib, feats = lax.optimization_barrier((sib, sources_sib, feats))
    table_sib, face_first = call(
        pack_first,
        (sds((width, half), bf16), sds((width, first), bf16)),
        sib, rest, share,
        flops=2 * width * half * first,
    )
    got_first = send(face_first, ring)
    feats_sib = send(feats, swap)
    face_last = call(
        pack_last, sds((width, last), bf16), table_sib, rest, share,
        flops=2 * width * half * last,
    )
    sources_sib, face_last = lax.optimization_barrier((sources_sib, face_last))
    pos_own, pos_sib, ahead = call(
        functools.partial(places, half, face, first, chunk),
        (
            sds(sources_own.shape, i32),
            sds(sources_own.shape, i32),
            sds((3, 2 * edges // chunk + 1), i32),
        ),
        block_counts.T, sources_own, sources_sib,
        smem=(0,), smem_out=(2,),
    )
    n_blocks = (2 * edges + BLK - 1) // BLK + 3
    grouped, wz, w1, w2 = call(
        group,
        (
            sds((2 * n_blocks + 2, FEATS, LANES), bf16),
            sds(w_zero.shape, bf16),
            sds((2 * w_one.shape[1],) * 2, bf16),
            sds((2 * w_two.shape[1],) * 2, bf16),
        ),
        ahead, feats, feats_sib, pos_own, pos_sib, w_zero, w_one, w_two,
        smem=(0,), hbm=(5, 6, 7), vmem=16,
        scratch=[pltpu.VMEM(a.shape, a.dtype) for a in (w_zero, w_one, w_two)]
        + [pltpu.SemaphoreType.DMA((3,))],
    )

    work = [
        pltpu.VMEM((width, BLK), f32),
        pltpu.VMEM((2, WROWS, BLK), f32),
        pltpu.VMEM((width, BLK), bf16),
        pltpu.VMEM((width, BLK), f32),
    ]
    scratch = [pltpu.VMEM((1, width, BLK), bf16)] + work
    half_sum = pltpu.VMEM((half, width), f32)
    near = call(
        functools.partial(sum_near, (0, NEAR_BLOCKS), lambda g: half * g),
        sds((slab, width), f32),
        ahead, grouped, table, wz, w1, w2,
        smem=(0,), scratch=scratch, vmem=20,
    )
    near, face_last = lax.optimization_barrier((near, face_last))
    got_last = send(face_last, ring)
    near = call(
        functools.partial(sum_more, 0, (NEAR_BLOCKS, ALL), lambda g: half * g),
        sds((slab, width), f32),
        ahead, grouped, table, wz, w1, w2, near,
        smem=(0,), scratch=scratch, vmem=20,
    )
    both = call(
        functools.partial(sum_more, 1, (0, ALL), lambda g: slab + face * g),
        sds((slab, width), f32),
        ahead, grouped, got_first, wz, w1, w2, near,
        smem=(0,), scratch=scratch, vmem=20,
    )
    theirs, msgs = call(
        functools.partial(sum_theirs, lambda g: slab + face * g + first),
        (
            sds((coefs, half, chan), bf16),
            sds(((2 * edges + BLK - 1) // BLK, width, BLK), bf16),
        ),
        ahead, grouped, got_last, wz, w1, w2, both,
        smem=(0,), scratch=[half_sum] + work, vmem=20,
    )
    got = send(theirs, swap)
    mine = call(
        sum_mine,
        sds((coefs, half, chan), f32),
        ahead, grouped, msgs, both,
        smem=(0,), scratch=[half_sum], vmem=20, flops=4 * BLK * width * half,
    )
    full = call(
        total_of,
        sds((coefs, half, chan), bf16),
        mine, got,
        hbm_out=True,
        scratch=[pltpu.VMEM((coefs, half, chan), bf16), pltpu.SemaphoreType.DMA((coefs,))],
    )
    return jnp.transpose(full, (1, 0, 2))


def solution(mesh):
    both = P(AXES)
    return jax.shard_map(
        per_device,
        mesh=mesh,
        in_specs=(
            P(AXES, None, None),
            P("slab", None, None),
            both,
            both,
            P(),
            P(None, AXES),
            P(AXES, None),
            P(),
            P(),
            P(),
        ),
        out_specs=P(AXES, None, None),
        check_vma=False,
    )
```

```python
import functools

import jax
import jax.numpy as jnp
from jax import lax
from jax.experimental import pallas as pl
from jax.experimental.pallas import tpu as pltpu
from jax.sharding import PartitionSpec as P

EDGE_BLOCK = 128
BLK = 256
LANES = 128
LAST_CHUNK = 256
STRIDE = 1 << 16
ALL = 1 << 16
NEAR_BLOCKS = 4
MESSAGE_SCALE = 0.2
WIGNER_BLOCKS = ((0, 0, 1), (1, 1, 3), (10, 4, 5))
ORDER = (0, 2, 6, 3, 7, 1, 5, 8, 4)
AXES = ("slab", "graph")
WROWS = 48
HI, LO, IDX, FEATS = 128, 176, 224, 256

f32, bf16, i32 = jnp.float32, jnp.bfloat16, jnp.int32


def nn(a, b):
    return lax.dot_general(a, b, (((1,), (0,)), ((), ())), preferred_element_type=f32)


def nt(a, b):
    return lax.dot_general(a, b, (((1,), (1,)), ((), ())), preferred_element_type=f32)


def hot(index, rows):
    return jnp.where(
        lax.broadcasted_iota(i32, (rows, index.shape[1]), 0) == index, 1.0, 0.0
    ).astype(bf16)


def call(body, out_shape, *args, smem=(), hbm=(), smem_out=(), hbm_out=False, scratch=(), flops=0, vmem=8):
    outs = out_shape if isinstance(out_shape, (tuple, list)) else (out_shape,)
    args = [
        pltpu.with_memory_space_constraint(a, pltpu.HBM) if i in hbm else a
        for i, a in enumerate(args)
    ]
    spec = lambda on: pl.BlockSpec(memory_space=pltpu.SMEM if on else pltpu.VMEM)
    size = sum(a.size * a.dtype.itemsize for a in (*args, *outs)) if flops else 0
    return pl.pallas_call(
        body,
        out_shape=out_shape,
        in_specs=[
            pl.BlockSpec(memory_space=pltpu.HBM) if i in hbm else spec(i in smem)
            for i in range(len(args))
        ],
        out_specs=[spec(i in smem_out) for i in range(len(outs))]
        if isinstance(out_shape, (tuple, list))
        else (pl.BlockSpec(memory_space=pltpu.HBM) if hbm_out else spec(0 in smem_out)),
        scratch_shapes=list(scratch),
        compiler_params=pltpu.CompilerParams(vmem_limit_bytes=vmem * 1024 * 1024),
        cost_estimate=pl.CostEstimate(flops=flops, bytes_accessed=size, transcendentals=0),
    )(*args)


def spot():
    return lax.axis_index("slab"), lax.axis_index("graph")


def listed(boundary, base):
    g = spot()[1]
    both = boundary[0]
    return jnp.where(g == 0, both[1:2], both[0:1]) - base


def transposed(rows, table):
    for c in range(rows.shape[0]):
        for i in range(0, rows.shape[1], LANES):
            table[c * LANES : (c + 1) * LANES, i : i + LANES] = rows[c, i : i + LANES, :].T


def pack_first(sib, rest, share, table, face):
    half, first = sib.shape[1], face.shape[1]
    transposed(sib, table)
    index = rest[:, 0:first]
    face[...] = (nn(table[...], hot(index, half)) + share[:, 0:first].astype(f32)).astype(bf16)


def pack_last(table, rest, share, face):
    half, first = table.shape[1], share.shape[1] - face.shape[1]
    index = rest[:, first:]
    face[...] = (nn(table[...], hot(index, half)) + share[:, first:].astype(f32)).astype(bf16)


def fetch(sources, targets, sems):
    copies = [
        pltpu.make_async_copy(src, dst, sems.at[i])
        for i, (src, dst) in enumerate(zip(sources, targets))
    ]
    for copy in copies:
        copy.start()
    return copies


def early(*refs):
    given, outs, held, (padded, sems) = refs[:6], refs[6:10], refs[10:16], refs[16:]
    table, share, rest, feats = outs
    copies = fetch(given, held, sems)
    own, boundary, radial, wigner, sources, targets = held
    half = own.shape[1]
    copies[0].wait()
    transposed(own, table)
    copies[1].wait()
    share[...] = nn(table[...], hot(listed(boundary, half * spot()[1]), half)).astype(bf16)
    rest[...] = listed(boundary, half - half * spot()[1])
    for copy in copies[2:]:
        copy.wait()
    chunks, _, size = feats.shape
    padded[...] = jnp.zeros(padded.shape, f32)
    padded[0 : wigner.shape[0], :] = wigner[...]
    row = lax.broadcasted_iota(i32, (FEATS - IDX, LANES), 0)
    for j in range(chunks):
        value = padded[:, j * size : (j + 1) * size]
        high = value.astype(bf16)
        feats[j, HI:LO, :] = high
        feats[j, LO:IDX, :] = (value - high.astype(f32)).astype(bf16)
        for i in range(0, size, LANES):
            at = j * size + i
            feats[j, 0:LANES, i : i + LANES] = radial[at : at + LANES, :].T
            src = sources[at // LANES : at // LANES + 1, :]
            tgt = targets[at // LANES : at // LANES + 1, :]
            digits = jnp.where(row == 0, src // 256, jnp.where(row == 1, src % 256, 0))
            digits = jnp.where(row == 2, tgt // 256, jnp.where(row == 3, tgt % 256, digits))
            feats[j, IDX:FEATS, i : i + LANES] = digits.astype(f32).astype(bf16)


def places(half, face, first, chunk, block_counts, own, sib, pos_own, pos_sib, ahead):
    s, g = spot()
    rows = own.shape[0]
    edge = lax.broadcasted_iota(i32, (rows, LANES), 0) * LANES + lax.broadcasted_iota(
        i32, (rows, LANES), 1
    )
    own_src = jnp.where(edge < block_counts[g, s] * EDGE_BLOCK, own[...], -1)
    sib_src = jnp.where(edge < block_counts[1 - g, s] * EDGE_BLOCK, sib[...], -1)
    src = jnp.concatenate([own_src, sib_src], axis=0)
    near = src - half * g
    at = src - 2 * half - face * g
    on_face = jnp.logical_and(at >= 0, at < face)
    masks = (
        jnp.logical_and(src >= 0, jnp.logical_and(near >= 0, near < half)),
        jnp.logical_and(on_face, at < first),
        jnp.logical_and(on_face, at >= first),
    )
    both = 2 * rows
    upper = (
        lax.broadcasted_iota(i32, (LANES, LANES), 0) < lax.broadcasted_iota(i32, (LANES, LANES), 1)
    ).astype(f32).astype(bf16)
    lower = (
        lax.broadcasted_iota(i32, (both, both), 1) < lax.broadcasted_iota(i32, (both, both), 0)
    ).astype(f32).astype(bf16)
    ones = jnp.ones((LANES, LANES), bf16)
    pos = jnp.full((both, LANES), -1, i32)
    step = chunk // LANES
    for k, mask in enumerate(masks):
        member = mask.astype(f32)
        m16 = member.astype(bf16)
        before = nn(nn(lower, m16).astype(bf16), ones) + nn(m16, upper)
        pos = jnp.where(mask, before.astype(i32) + k * STRIDE, pos)
        total = 0
        for j in range(both // step):
            ahead[k, j] = total
            total = total + jnp.sum(member[j * step : (j + 1) * step]).astype(i32)
        ahead[k, both // step] = total
    pos_own[...] = pos[0:rows]
    pos_sib[...] = pos[rows:both]


def blocks_of(ahead):
    return [(ahead[k, ahead.shape[1] - 1] + (BLK - 1)) // BLK for k in range(3)]


def group(
    ahead, feat_own, feat_sib, pos_own, pos_sib, zero_given, one_given, two_given,
    out, wz, w1, w2,
    w_zero, w_one, w_two, sems,
):
    copies = fetch((zero_given, one_given, two_given), (w_zero, w_one, w_two), sems)
    n = blocks_of(ahead)
    chunks, _, size = feat_own.shape
    per = size // LANES
    first_tile = [0, 2 * n[0], 2 * (n[0] + n[1])]
    out[...] = jnp.zeros(out.shape, bf16)
    row = lax.broadcasted_iota(i32, (BLK, LANES), 0)

    for part, (feat, pos) in enumerate(((feat_own, pos_own), (feat_sib, pos_sib))):

        def add(j, k, low_tile, picked_rows):
            want = row + (low_tile * LANES + k * STRIDE)
            mask = jnp.concatenate(
                [jnp.where(r == want, 1.0, 0.0).astype(bf16) for r in picked_rows], axis=1
            )
            picked = nt(feat[j], mask).astype(bf16)
            for i in range(2):
                t = first_tile[k] + low_tile + i
                out[t] = out[t] + picked[:, i * LANES : (i + 1) * LANES]

        def one_chunk(j, carry):
            rows = [pos[pl.ds(j * per + i, 1), :] for i in range(per)]
            low = [ahead[k, part * chunks + j] // LANES for k in range(3)]
            for k in range(3):
                add(j, k, low[k], rows)
            for k in range(3):
                high = (ahead[k, part * chunks + j + 1] + (LANES - 1)) // LANES
                more = (high - low[k] + 1) // 2

                def again(i, carry):
                    add(j, k, low[k] + 2 * i, rows)
                    return carry

                lax.fori_loop(1, more, again, 0)
            return carry

        lax.fori_loop(0, chunks, one_chunk, 0)

    for copy in copies:
        copy.wait()
    wz[...] = w_zero[...].T
    for weights, out in ((w_one, w1), (w_two, w2)):
        n = weights.shape[1]
        real, imag = weights[0].T, weights[1].T
        out[0:n, 0:n] = real
        out[0:n, n : 2 * n] = (-imag.astype(f32)).astype(bf16)
        out[n : 2 * n, 0:n] = imag
        out[n : 2 * n, n : 2 * n] = real


def features_of(grouped, block, low, high):
    tiles = [grouped[2 * block + i, low:high, :].astype(f32) for i in range(2)]
    return jnp.concatenate(tiles, axis=1)


def number(grouped, block, row):
    digits = features_of(grouped, block, IDX, IDX + 16)
    return (digits[row : row + 1] * 256.0 + digits[row + 1 : row + 2]).astype(i32)


def mask_of(grouped, block, half, base, rows):
    tgt = number(grouped, block, 2) + half * spot()[1]
    return hot(jnp.where(tgt >= 2 * half, tgt - 2 * half, tgt) - base, rows)


def messages_of(
    kind, part, shift, ahead, grouped, table, wz, w1, w2, begin, spread, end, msgs, x, w, rot, mix
):
    n = blocks_of(ahead)
    start = (0, n[0], n[0] + n[1])[kind] + part[0]
    n = jnp.minimum(jnp.maximum(n[kind] - part[0], 0), part[1])
    g = spot()[1]
    rows = table.shape[1]
    n_zero, n_one = wz.shape[0], w1.shape[0]
    slot = {c: i for i, c in enumerate(ORDER)}

    feature = lambda b, low, high: features_of(grouped, start + b, low, high)
    slot_of = lambda b: b if msgs.shape[0] > 1 else 0

    def gather(b):
        w[b % 2] = feature(b, HI, LO) + feature(b, LO, IDX)
        x[...] = nn(table[...], hot(number(grouped, start + b, 0) - shift(g), rows))

    def turn(b, source, at, inverse, q):
        for offset, first, size in WIGNER_BLOCKS:
            for i in range(size):
                total = None
                for j in range(size):
                    k = offset + (j * size + i if inverse else i * size + j)
                    r = at(first + j) * LANES + q
                    term = w[b % 2, k : k + 1, :] * source[r : r + 16, :]
                    total = term if total is None else total + term
                yield first + i, total

    def forth(b):
        for q in range(0, LANES, 16):
            rad = feature(b, q, q + 16)
            for c, total in turn(b, x, lambda c: c, False, q):
                r = slot[c] * LANES + q
                rot[r : r + 16, :] = (total * rad).astype(bf16)

    def blend():
        mix[0:n_zero, :] = nn(wz[...], rot[0:n_zero, :])
        mix[n_zero : n_zero + n_one, :] = nn(w1[...], rot[n_zero : n_zero + n_one, :])
        mix[n_zero + n_one :, :] = nn(w2[...], rot[n_zero + n_one :, :])

    def back(b):
        for q in range(0, LANES, 16):
            for c, total in turn(b, mix, lambda c: slot[c], True, q):
                r = c * LANES + q
                msgs[slot_of(b), r : r + 16, :] = total.astype(bf16)

    @pl.when(n > 0)
    def _():
        begin()
        gather(0)
        forth(0)
        blend()

        def one(b, carry):
            gather(b)
            back(b - 1)
            forth(b)
            spread(start + b - 1, slot_of(b - 1))
            blend()
            return carry

        lax.fori_loop(1, n, one, 0)
        back(n - 1)
        end(start + n - 1, slot_of(n - 1))

    @pl.when(n == 0)
    def _():
        begin()
        end(None, 0)


def add_to(acc, grouped, msgs, base=0):
    half = acc.shape[0] if base else acc.shape[0] // 2

    def spread(block, at):
        acc[...] += nt(mask_of(grouped, block, half, base, acc.shape[0]), msgs[at])

    def end(block, at):
        if block is not None:
            spread(block, at)

    return spread, end


def sum_near(part, shift, ahead, grouped, table, wz, w1, w2, acc, msgs, *scratch):
    def begin():
        acc[...] = jnp.zeros(acc.shape, f32)

    spread, end = add_to(acc, grouped, msgs)
    messages_of(
        0, part, shift, ahead, grouped, table, wz, w1, w2, begin, spread, end, msgs, *scratch
    )


def sum_more(kind, part, shift, ahead, grouped, table, wz, w1, w2, before, acc, msgs, *scratch):
    def begin():
        acc[...] = before[...]

    spread, end = add_to(acc, grouped, msgs)
    messages_of(
        kind, part, shift, ahead, grouped, table, wz, w1, w2, begin, spread, end, msgs, *scratch
    )


def sum_theirs(shift, ahead, grouped, table, wz, w1, w2, before, theirs, msgs, acc, *scratch):
    half, width = acc.shape

    def begin():
        acc[...] = before[half:, :]

    spread = add_to(acc, grouped, msgs, half)[0]

    def end(block, at):
        for r in range(0, width, 2 * LANES):
            step = min(2 * LANES, width - r)
            part = acc[:, r : r + step]
            if block is not None:
                mask = mask_of(grouped, block, half, half, half)
                part = part + nt(mask, msgs[at, r : r + step, :])
            for c in range(step // LANES):
                theirs[r // LANES + c] = part[:, c * LANES : (c + 1) * LANES].astype(bf16)

    messages_of(
        2, (0, ALL), shift, ahead, grouped, table, wz, w1, w2, begin, spread, end, msgs, *scratch
    )


def sum_mine(ahead, grouped, msgs, before, mine, acc):
    half = acc.shape[0]
    n = blocks_of(ahead)
    acc[...] = before[0:half, :]

    def one(b, carry):
        acc[...] += nt(mask_of(grouped, n[0] + n[1] + b, half, 0, half), msgs[b])
        return carry

    lax.fori_loop(0, n[2], one, 0)
    for c in range(mine.shape[0]):
        mine[c] = acc[:, c * LANES : (c + 1) * LANES]


def total_of(mine, theirs, out, held, sems):
    copies = []
    for c in range(mine.shape[0]):
        value = (mine[c] + theirs[c].astype(f32)) * MESSAGE_SCALE
        held[c] = value.astype(bf16)
        copies.append(pltpu.make_async_copy(held.at[c], out.at[c], sems.at[c]))
        copies[-1].start()
    for copy in copies:
        copy.wait()


def per_device(
    nodes, boundary, sources, targets, block_counts, wigner, radial, w_zero, w_one, w_two
):
    half, coefs, chan = nodes.shape
    slab, width = 2 * half, coefs * chan
    face = boundary.shape[2]
    last = min(LAST_CHUNK, face // 2)
    first = face - last
    edges = sources.shape[0]
    chunk = next(c for c in (512, 256, LANES) if edges % c == 0)
    n_slab = lax.axis_size("slab")
    sds = jax.ShapeDtypeStruct

    place = lambda i, j: (i % n_slab) * 2 + j
    swap = [(place(i, j), place(i, 1 - j)) for i in range(n_slab) for j in range(2)]
    ring = [(place(i, 0), place(i + 1, 0)) for i in range(n_slab)]
    ring += [(place(i, 1), place(i - 1, 1)) for i in range(n_slab)]
    send = lambda x, to: lax.ppermute(x, AXES, to)

    own = jnp.transpose(nodes, (1, 0, 2))
    sib = send(own, swap)
    sources_own = sources.reshape(-1, LANES)
    sources_sib = send(sources_own, swap)

    given = (own, boundary, radial, wigner, sources_own, targets.reshape(-1, LANES))
    table, share, rest, feats = call(
        early,
        (
            sds((width, half), bf16),
            sds((width, face), bf16),
            sds((1, face), i32),
            sds((edges // chunk, FEATS, chunk), bf16),
        ),
        *given,
        hbm=range(6), vmem=16,
        scratch=[pltpu.VMEM(a.shape, a.dtype) for a in given]
        + [pltpu.VMEM((WROWS, edges), f32), pltpu.SemaphoreType.DMA((6,))],
    )
    sib, sources_sib, feats = lax.optimization_barrier((sib, sources_sib, feats))
    table_sib, face_first = call(
        pack_first,
        (sds((width, half), bf16), sds((width, first), bf16)),
        sib, rest, share,
        flops=2 * width * half * first,
    )
    got_first = send(face_first, ring)
    feats_sib = send(feats, swap)
    face_last = call(
        pack_last, sds((width, last), bf16), table_sib, rest, share,
        flops=2 * width * half * last,
    )
    sources_sib, face_last = lax.optimization_barrier((sources_sib, face_last))
    pos_own, pos_sib, ahead = call(
        functools.partial(places, half, face, first, chunk),
        (
            sds(sources_own.shape, i32),
            sds(sources_own.shape, i32),
            sds((3, 2 * edges // chunk + 1), i32),
        ),
        block_counts.T, sources_own, sources_sib,
        smem=(0,), smem_out=(2,),
    )
    n_blocks = (2 * edges + BLK - 1) // BLK + 3
    grouped, wz, w1, w2 = call(
        group,
        (
            sds((2 * n_blocks + 2, FEATS, LANES), bf16),
            sds(w_zero.shape, bf16),
            sds((2 * w_one.shape[1],) * 2, bf16),
            sds((2 * w_two.shape[1],) * 2, bf16),
        ),
        ahead, feats, feats_sib, pos_own, pos_sib, w_zero, w_one, w_two,
        smem=(0,), hbm=(5, 6, 7), vmem=16,
        scratch=[pltpu.VMEM(a.shape, a.dtype) for a in (w_zero, w_one, w_two)]
        + [pltpu.SemaphoreType.DMA((3,))],
    )

    work = [
        pltpu.VMEM((width, BLK), f32),
        pltpu.VMEM((2, WROWS, BLK), f32),
        pltpu.VMEM((width, BLK), bf16),
        pltpu.VMEM((width, BLK), f32),
    ]
    scratch = [pltpu.VMEM((1, width, BLK), bf16)] + work
    half_sum = pltpu.VMEM((half, width), f32)
    near = call(
        functools.partial(sum_near, (0, NEAR_BLOCKS), lambda g: half * g),
        sds((slab, width), f32),
        ahead, grouped, table, wz, w1, w2,
        smem=(0,), scratch=scratch, vmem=20,
    )
    near, face_last = lax.optimization_barrier((near, face_last))
    got_last = send(face_last, ring)
    near = call(
        functools.partial(sum_more, 0, (NEAR_BLOCKS, ALL), lambda g: half * g),
        sds((slab, width), f32),
        ahead, grouped, table, wz, w1, w2, near,
        smem=(0,), scratch=scratch, vmem=20,
    )
    both = call(
        functools.partial(sum_more, 1, (0, ALL), lambda g: slab + face * g),
        sds((slab, width), f32),
        ahead, grouped, got_first, wz, w1, w2, near,
        smem=(0,), scratch=scratch, vmem=20,
    )
    theirs, msgs = call(
        functools.partial(sum_theirs, lambda g: slab + face * g + first),
        (
            sds((coefs, half, chan), bf16),
            sds(((2 * edges + BLK - 1) // BLK, width, BLK), bf16),
        ),
        ahead, grouped, got_last, wz, w1, w2, both,
        smem=(0,), scratch=[half_sum] + work, vmem=20,
    )
    got = send(theirs, swap)
    mine = call(
        sum_mine,
        sds((coefs, half, chan), f32),
        ahead, grouped, msgs, both,
        smem=(0,), scratch=[half_sum], vmem=20, flops=4 * BLK * width * half,
    )
    full = call(
        total_of,
        sds((coefs, half, chan), bf16),
        mine, got,
        hbm_out=True,
        scratch=[pltpu.VMEM((coefs, half, chan), bf16), pltpu.SemaphoreType.DMA((coefs,))],
    )
    return jnp.transpose(full, (1, 0, 2))


def solution(mesh):
    both = P(AXES)
    return jax.shard_map(
        per_device,
        mesh=mesh,
        in_specs=(
            P(AXES, None, None),
            P("slab", None, None),
            both,
            both,
            P(),
            P(None, AXES),
            P(AXES, None),
            P(),
            P(),
            P(),
        ),
        out_specs=P(AXES, None, None),
        check_vma=False,
    )
```
